128 devices in a mesh: pipe: 4 (over x_lo, core), tensor: 8 (over z, x_hi), dp: 4 (over y).
Axes of the slice: x: 4 (x_hi: 2, x_lo: 2; x = x_hi * 2 + x_lo), y: 4, z: 4, core: 2. Of those that a mesh axis runs over, the one named last changes fastest.
Arguments:
- cotangent: bfloat16 [8, 192, 4096], P('dp', 'tensor'), may hold values from -6 to 6
- saved_u: bfloat16 [4, 8, 192, 12288], P('pipe', 'dp', None, 'tensor'), may hold values from -3 to 3
- dt_raw: float32 [4, 8, 192, 128], P('pipe', 'dp', None, 'tensor'), may hold values from -5 to 5
- in_weight: bfloat16 [4, 4096, 12288], P('pipe', None, 'tensor'), may hold values from -0.0390625 to 0.0390625
- out_weight: bfloat16 [4, 8192, 4096], P('pipe', 'tensor'), may hold values from -0.0625 to 0.0625
- conv_weight: float32 [4, 4, 12288], P('pipe', None, 'tensor'), may hold values from -3 to 3
- conv_bias: float32 [4, 12288], P('pipe', 'tensor'), may hold values from -3 to 3
- a_log: float32 [4, 128], P('pipe', 'tensor'), may hold values from -5.5 to 0
- dt_bias: float32 [4, 128], P('pipe', 'tensor'), may hold values from -5 to -2
- d_skip: float32 [4, 128], P('pipe', 'tensor'), may hold values from 0.5 to 1.5
Outputs:
- grad_input: bfloat16 [4, 8, 192, 4096], P('pipe', 'dp', 'tensor')
- grad_out_weight: bfloat16 [4, 8192, 4096], P('pipe', 'tensor', 'dp')
- grad_conv_weight: float32 [4, 4, 12288], P('pipe', None, 'tensor')
- grad_conv_bias: float32 [4, 12288], P('pipe', 'tensor')
- grad_a_log: float32 [4, 128], P('pipe', 'tensor')
- grad_dt_bias: float32 [4, 128], P('pipe', 'tensor')
- grad_d_skip: float32 [4, 128], P('pipe', 'tensor')
The draws below stay inside these ranges and needn't reach their ends.
All inputs are finite; a program needn't handle non-finite values.
Results may differ from the reference program's by a relative error of at most 0.025.
Values may be sent and summed in bfloat16 or wider, within the bound.
A program may use at most 192 MiB of HBM per device.

```python
import jax
import jax.numpy as jnp
from jax import lax

D = 4096
HEADS = 128
HEAD_DIM = 64
GROUPS = 8
STATE = 256
KW = 4
SEQ = 192
LAYERS = 4
BATCH = 8
DIN = 8192
CONV = 12288


def draw_a_log(key, part):
    key = jax.random.fold_in(key, 11)
    return jax.random.uniform(key, (LAYERS, HEADS), jnp.float32, -3.0, 0.0)


def draw_dt_bias(key, part):
    key = jax.random.fold_in(key, 12)
    return jax.random.uniform(key, (LAYERS, HEADS), jnp.float32, -5.0, -2.0)


def levels(own_key, dims, cuts, low, high):
    def one(axis_at, blocks):
        draws = jax.random.uniform(jax.random.fold_in(jax.random.fold_in(own_key, 6), axis_at), (blocks,), jnp.float32, low / len(cuts), high / len(cuts))
        return jnp.repeat(jnp.exp(draws), dims[axis_at] // blocks).reshape((-1,) + (1,) * (len(dims) - axis_at - 1))

    level = one(*cuts[0])
    for cut in cuts[1:]:
        level = level * one(*cut)
    return level


def noise(stream_key, extent, scale, bound, cuts=(), held_as=jnp.bfloat16):
    loudness = levels(stream_key, extent, cuts, -0.22, 0.18) if cuts else 1.0
    result = jax.random.normal(stream_key, extent, jnp.float32) * scale * loudness
    return jnp.minimum(jnp.maximum(result, -bound), bound).astype(held_as)


def setup_inputs(seed: int = 0) -> dict:
    key_of = jax.random.split(jax.random.key(seed), 11)
    cotangent = noise(key_of[0], (BATCH, SEQ, D), 1.0, 6.0, ((0, 4), (1, 8)))
    saved_u = noise(key_of[1], (LAYERS, BATCH, SEQ, CONV), 0.5, 3.0, ((0, 4), (1, 4), (3, 8)))
    dt_raw = noise(key_of[2], (LAYERS, BATCH, SEQ, HEADS), 1.0, 5.0, ((0, 4), (1, 4), (3, 8)), jnp.float32)
    in_weight = noise(key_of[3], (LAYERS, D, CONV), (2 * CONV) ** -0.5, 0.0390625, ((0, 4), (2, 8)))
    out_weight = noise(key_of[4], (LAYERS, DIN, D), DIN ** -0.5, 0.0625, ((0, 4), (1, 8)))
    conv_weight = noise(key_of[5], (LAYERS, KW, CONV), KW ** -0.5, 3.0, ((0, 4), (2, 8)), jnp.float32)
    conv_bias = noise(key_of[6], (LAYERS, CONV), 0.5, 3.0, ((0, 4), (1, 8)), jnp.float32)
    a_log = draw_a_log(jax.random.fold_in(key_of[10], 71), 0)
    dt_bias = draw_dt_bias(jax.random.fold_in(key_of[10], 71), 0)
    d_skip = jnp.clip(0.5 + 1.0 * jax.random.uniform(key_of[9], (LAYERS, HEADS), jnp.float32) ** levels(key_of[9], (LAYERS, HEADS), ((0, 4), (1, 8)), -0.2, 0.2), 0.5, 1.5)
    return {"cotangent": cotangent, "saved_u": saved_u, "dt_raw": dt_raw, "in_weight": in_weight, "out_weight": out_weight, "conv_weight": conv_weight, "conv_bias": conv_bias, "a_log": a_log, "dt_bias": dt_bias, "d_skip": d_skip}


HIGHEST_PRECISION = lax.Precision.HIGHEST

def mix_forward(inputs, raw_steps, taps, tap_bias, log_rates, step_bias, skip_gain, group_count):
    length = inputs.shape[0]
    width = taps.shape[0]
    padded = jnp.pad(inputs, ((width - 1, 0), (0, 0)))
    mixed = jnp.broadcast_to(tap_bias, inputs.shape)
    for offset in range(width):
        mixed = mixed + taps[offset] * padded[offset:offset + length]
    active = jax.nn.silu(mixed).reshape(length, group_count, -1)
    inner = active.shape[2] - 2 * STATE
    per_group = inner // HEAD_DIM
    values = active[:, :, :inner].reshape(length, group_count, per_group, HEAD_DIM)
    keys_b = active[:, :, inner:inner + STATE]
    query_c = active[:, :, inner + STATE:]
    deltas = jax.nn.softplus(raw_steps + step_bias).reshape(length, group_count, per_group)
    rates = -jnp.exp(log_rates).reshape(group_count, per_group)
    totals = jnp.cumsum(deltas * rates, axis=0)
    causal = (jnp.arange(length)[:, None] >= jnp.arange(length)[None, :])[:, :, None, None]
    spread = totals[:, None] - totals[None, :]
    decay = jnp.where(causal, jnp.exp(jnp.where(causal, spread, 0.0)), 0.0)
    intersection = jnp.einsum('tgn,sgn->tsg', query_c, keys_b, precision=HIGHEST_PRECISION)
    mixing = decay * intersection[:, :, :, None] * deltas[None]
    output = jnp.einsum('tsgh,sghp->tghp', mixing, values, precision=HIGHEST_PRECISION)
    output = output + skip_gain.reshape(group_count, per_group)[None, :, :, None] * values
    return output.reshape(length, -1)

def reference(cotangent, saved_u, dt_raw, in_weight, out_weight, conv_weight, conv_bias, a_log, dt_bias, d_skip):
    current = [cotangent[index] for index in range(BATCH)]
    input_grads = [None] * LAYERS
    weight_grads = [None] * LAYERS
    small_grads = [None] * LAYERS
    for section_no in range(LAYERS - 1, -1, -1):
        weight_total = jnp.zeros((DIN, D), jnp.float32)
        small = (jnp.zeros((KW, CONV), jnp.float32), jnp.zeros((CONV,), jnp.float32), jnp.zeros((HEADS,), jnp.float32), jnp.zeros((HEADS,), jnp.float32), jnp.zeros((HEADS,), jnp.float32))
        upward = []
        for seq_no in range(BATCH):
            grad_now = current[seq_no]
            raw_now = dt_raw[section_no, seq_no]

            def forward(inputs, taps, tap_bias, log_rates, step_bias, skip_gain):
                return mix_forward(inputs, raw_now, taps, tap_bias, log_rates, step_bias, skip_gain, GROUPS)
            output, pull = jax.vjp(forward, saved_u[section_no, seq_no].astype(jnp.float32), conv_weight[section_no], conv_bias[section_no], a_log[section_no], dt_bias[section_no], d_skip[section_no])
            output_low = output.astype(jnp.bfloat16)
            weight_total = weight_total + jnp.dot(output_low.T, grad_now, preferred_element_type=jnp.float32)
            grad_mix = jnp.dot(grad_now, out_weight[section_no].T, preferred_element_type=jnp.float32).astype(jnp.bfloat16)
            pulled = pull(lax.optimization_barrier(grad_mix).astype(jnp.float32))
            grad_inputs = pulled[0].astype(jnp.bfloat16)
            total = jnp.dot(grad_inputs, in_weight[section_no].T, preferred_element_type=jnp.float32)
            upward.append((grad_now.astype(jnp.float32) + total).astype(jnp.bfloat16))
            small = tuple((old + new for old, new in zip(small, pulled[1:])))
        input_grads[section_no] = jnp.stack(upward)
        weight_grads[section_no] = weight_total.astype(jnp.bfloat16)
        small_grads[section_no] = small
        current = upward
    return (jnp.stack(input_grads), jnp.stack(weight_grads), jnp.stack([entry[0] for entry in small_grads]), jnp.stack([entry[1] for entry in small_grads]), jnp.stack([entry[2] for entry in small_grads]), jnp.stack([entry[3] for entry in small_grads]), jnp.stack([entry[4] for entry in small_grads]))
```

```python
import jax
import jax.numpy as jnp
from jax import lax
from jax.experimental import pallas as pl
from jax.experimental.pallas import tpu as pltpu
from jax.sharding import PartitionSpec as P

F32 = jnp.float32
BF16 = jnp.bfloat16
MESH = pl.DeviceIdType.MESH
NT = (((1,), (1,)), ((), ()))
NN = (((1,), (0,)), ((), ()))
TN = (((0,), (0,)), ((), ()))
HIGH = lax.Precision.HIGHEST

L = 192
D = 4096
X = 1024
C = 1536
HEADS = 16
PAIRS = 8
N = 256
T = 8
W = D // T
R = L // T
DP = 4
S = 2
TOP = 8


def dot(a, b, dims, precision=None):
    return lax.dot_general(a, b, dims, preferred_element_type=F32, precision=precision)


def iota(shape, axis):
    return lax.broadcasted_iota(jnp.int32, shape, axis)


def lanes(j, width=128):
    return pl.ds(pl.multiple_of(j * width, width), width)


def loop(count, body):
    def step(i, carry):
        body(i)
        return carry

    lax.fori_loop(0, count, step, 0)


def kernel(
    cot_ref, u_hbm, win_hbm, wout_hbm, dtr_ref, cw_ref, cb_ref, al_ref, db_ref, sk_ref,
    gi_out, gow_out, pg_out,
    win, wout, u_ref, upad, sp, abf, xst, mt, est, y0, yb, sT, scol, dtc, skl,
    cbuf, crecv, gbuf, gcols, dyacc, dybf, dx0, dcb, dcpad, dubf, own,
    sbuf, rbuf, opart, obuf, girecv, gi_v, pg, pgr, pgsum,
    loc, cs_s, cs_r, g_s, g_r, rs_s, rs_r, ox_s, ox_r, yb_s, yb_r, gx_s, gx_r, pg_s, pg_r,
):
    p = lax.axis_index("pipe")
    t = lax.axis_index("tensor")
    d = lax.axis_index("dp")
    first = p == 3
    last = p == 0

    def peer(i):
        return (p, lax.rem(t + i, T), d)

    def replica(i):
        return (p, t, lax.rem(d + i, DP))

    def local(src, dst, i):
        return pltpu.make_async_copy(src, dst, loc.at[i])

    def remote(src, dst, ssem, rsem, to):
        return pltpu.make_async_remote_copy(
            src_ref=src, dst_ref=dst, send_sem=ssem, recv_sem=rsem, device_id=to, device_id_type=MESH
        )

    local(u_hbm, u_ref, 0).start()
    local(wout_hbm, wout, 1).start()
    local(win_hbm, win, 2).start()

    barrier = pltpu.get_barrier_semaphore()
    for i in range(1, T):
        pl.semaphore_signal(barrier, inc=1, device_id=peer(i), device_id_type=MESH)
    for i in range(1, DP):
        pl.semaphore_signal(barrier, inc=1, device_id=replica(i), device_id_type=MESH)

    @pl.when(p > 0)
    def _():
        for i in range(T):
            pl.semaphore_signal(barrier, inc=1, device_id=(p - 1, i, d), device_id_type=MESH)

    @pl.when(p < 3)
    def _():
        for i in range(T):
            pl.semaphore_signal(barrier, inc=1, device_id=(p + 1, i, d), device_id_type=MESH)

    middle = jnp.logical_and(p > 0, p < 3)

    @pl.when(middle)
    def _():
        pl.semaphore_wait(barrier, T - 1 + DP - 1 + 2 * T)

    @pl.when(jnp.logical_not(middle))
    def _():
        pl.semaphore_wait(barrier, T - 1 + DP - 1 + T)

    def cot_copy(s, i):
        return remote(cbuf.at[s], crecv.at[s, t], cs_s.at[s, i - 1], cs_r.at[s, i - 1], peer(i))

    def cot_arrival(s, i):
        src = lax.rem(t + T - i, T)
        return remote(cbuf.at[s], crecv.at[s, src], cs_s.at[s, i - 1], cs_r.at[s, i - 1], peer(i))

    @pl.when(first)
    def _():
        for s in range(S):
            cbuf[s] = cot_ref[s]
            for i in range(1, T):
                cot_copy(s, i).start()
            crecv[s, t] = cot_ref[s]

    rr = iota((L, L), 0)
    tt = iota((L, L), 1)
    lower = (rr >= tt).astype(F32)
    upper = (rr <= tt).astype(F32)
    rate = -jnp.exp(al_ref[...])
    spread = (iota((HEADS, X), 0) == iota((HEADS, X), 1) // 64).astype(F32)
    skl[...] = dot(sk_ref[...], spread, NN, HIGH)

    def forward(s):
        upad[s, 0:TOP, :] = jnp.zeros((TOP, C), F32)

        def conv(j):
            at = lanes(j)
            upad[s, TOP : TOP + L, at] = u_ref[s, :, at].astype(F32)
            c = jnp.broadcast_to(cb_ref[:, at], (L, 128))
            for k in range(4):
                c = c + cw_ref[k : k + 1, at] * upad[s, TOP - 3 + k : TOP - 3 + k + L, at]
            sig = 1.0 / (1.0 + jnp.exp(-c))
            sp[s, :, at] = sig * (1.0 + c * (1.0 - sig))
            abf[s, :, at] = (c * sig).astype(BF16)

        loop(C // 128, conv)
        z = dtr_ref[s] + db_ref[...]
        dt = jnp.maximum(z, 0.0) + jnp.log1p(jnp.exp(-jnp.abs(z)))
        dtc[s] = dt
        dta = dt * rate
        scol[...] = dot(lower, dta, NN, HIGH)
        sT[...] = dot(dta, upper, TN, HIGH)
        dcb[...] = dot(abf[s, :, X : X + N], abf[s, :, X + N : X + 2 * N], NT)

        def pair(j):
            at = lanes(j)
            x2 = abf[s, :, at].astype(F32)
            even = iota((L, 128), 1) < 64
            xst[s, j, 0:L, :] = jnp.where(even, x2, 0.0).astype(BF16)
            xst[s, j, L : 2 * L, :] = jnp.where(even, 0.0, x2).astype(BF16)
            causal = iota((L, L), 1) >= iota((L, L), 0)
            head = iota((L, HEADS), 1)
            for e in range(2):
                h = 2 * j + e
                s_r = jnp.sum(jnp.where(head == h, scol[...], 0.0), axis=1, keepdims=True)
                dt_r = jnp.sum(jnp.where(head == h, dtc[s], 0.0), axis=1, keepdims=True)
                decay = jnp.exp(jnp.minimum(sT[pl.ds(h, 1), :] - s_r, 0.0)) * dt_r
                decay = jnp.where(causal, decay, 0.0)
                est[s, j, e * L : (e + 1) * L, :] = decay.astype(BF16)
                mt[s, j, e * L : (e + 1) * L, :] = (decay * dcb[...]).astype(BF16)
            y2 = dot(mt[s, j], xst[s, j], TN)
            y0[s, :, at] = y2
            yb[d, s, :, at] = (y2 + skl[:, at] * x2).astype(BF16)

        loop(PAIRS, pair)

    def yb_copy(s, i):
        return remote(yb.at[d, s], yb.at[d, s], yb_s.at[s, i - 1], yb_r.at[s, i - 1], replica(i))

    def yb_arrival(s, i):
        src = lax.rem(d + DP - i, DP)
        return remote(yb.at[src, s], yb.at[src, s], yb_s.at[s, i - 1], yb_r.at[s, i - 1], replica(i))

    local(u_hbm, u_ref, 0).wait()
    for s in range(S):
        forward(s)
        for i in range(1, DP):
            yb_copy(s, i).start()

    local(wout_hbm, wout, 1).wait()
    local(win_hbm, win, 2).wait()

    def g_arrival(s, k):
        return remote(gbuf.at[s, k], gbuf.at[s, k], g_s.at[s, 0], g_r.at[s, k], peer(1))

    def gx_copy(s, i):
        to = lax.rem(d + i, DP)
        return remote(
            gbuf.at[s, pl.ds(2 * to, 2)], gcols.at[d, s], gx_s.at[s, i - 1], gx_r.at[s, i - 1], replica(i)
        )

    def gx_arrival(s, i):
        src = lax.rem(d + DP - i, DP)
        return remote(
            gbuf.at[s, pl.ds(0, 2)], gcols.at[src, s], gx_s.at[s, i - 1], gx_r.at[s, i - 1], replica(i)
        )

    def grad_mix(s):
        @pl.when(first)
        def _():
            for i in range(1, T):
                cot_arrival(s, i).wait_recv()

            def block(k):
                rows = crecv[s, :, :, lanes(k, W)].astype(F32)
                gbuf[s, k] = rows.reshape(L, W).astype(BF16)

            loop(T, block)

        dyacc[...] = jnp.zeros_like(dyacc)

        def block(i):
            k = lax.rem(t + i, T)

            @pl.when(p < 3)
            def _():
                g_arrival(s, k).wait_recv()

            dyacc[...] += dot(gbuf[s, k], wout[:, lanes(k, W)], NT)

        loop(T, block)
        dybf[...] = dyacc[...].astype(BF16)
        for i in range(1, DP):
            gx_copy(s, i).start()
        gcols[d, s] = gbuf[s, pl.ds(2 * d, 2)]

    def pull(s):
        dcb[...] = jnp.zeros_like(dcb)

        def pair(j):
            at = lanes(j)
            dy2 = dybf[:, at]
            dm = dot(xst[s, j], dy2, NT)
            dcb[...] += dm[:L] * est[s, j, 0:L, :].astype(F32) + dm[L:] * est[s, j, L : 2 * L, :].astype(F32)
            dx = dot(mt[s, j], dy2, NN)
            dx = jnp.where(iota((L, 128), 1) < 64, dx[:L], dx[L:])
            dx0[:, at] = dx
            dcpad[0:L, at] = (dx + skl[:, at] * dy2.astype(F32)) * sp[s, :, at]

        loop(PAIRS, pair)
        low = dcb[...].astype(BF16)
        dcpad[0:L, X : X + N] = dot(low, abf[s, :, X + N : X + 2 * N], NN) * sp[s, :, X : X + N]
        dcpad[0:L, X + N : X + 2 * N] = (
            dot(low, abf[s, :, X : X + N], TN) * sp[s, :, X + N : X + 2 * N]
        )

        def conv(j):
            at = lanes(j)
            du = cw_ref[3:4, at] * dcpad[0:L, at]
            for k in range(3):
                du = du + cw_ref[k : k + 1, at] * dcpad[3 - k : 3 - k + L, at]
            dubf[:, at] = du.astype(BF16)

        loop(C // 128, conv)

    def rs_copy(s, j):
        return remote(sbuf.at[j], rbuf.at[s, j], rs_s.at[s, j], rs_r.at[s, j], peer(1 + j))

    def scatter(s):
        def block(j):
            k = lax.rem(t + 1 + j, T)
            part = dot(dubf[...], win[lanes(k, W), :], NT)
            sbuf[j] = part.astype(BF16)
            rs_copy(s, j).start()

        loop(T - 1, block)
        own[...] = dot(dubf[...], win[lanes(t, W), :], NT)

    def g_copy(s, i):
        return remote(opart.at[s], gbuf.at[s, t], g_s.at[s, i], g_r.at[s, t], (p - 1, i, d))

    def ox_copy(s, i):
        return remote(
            obuf.at[s, lax.rem(t + i, T)], girecv.at[s, t], ox_s.at[s, i - 1], ox_r.at[s, i - 1], peer(i)
        )

    def ox_arrival(s, i):
        src = lax.rem(t + T - i, T)
        return remote(obuf.at[s, src], girecv.at[s, src], ox_s.at[s, i - 1], ox_r.at[s, i - 1], peer(i))

    def reduce(s):
        loop(T - 1, lambda j: rs_copy(s, j).wait_recv())

        def block(j):
            at = lanes(j)
            total = own[:, at] + gbuf[s, t, :, at].astype(F32)
            for i in range(T - 1):
                total = total + rbuf[s, i, :, at].astype(F32)
            opart[s, :, at] = total.astype(BF16)
            obuf[s, :, :, at] = total.reshape(T, R, 128).astype(BF16)

        loop(W // 128, block)

        @pl.when(p > 0)
        def _():
            for i in range(T):
                g_copy(s, i).start()

        for i in range(1, T):
            ox_copy(s, i).start()
        girecv[s, t] = obuf[s, t]
        loop(T - 1, lambda j: rs_copy(s, j).wait_send())

    def parameters(s):
        def two(value):
            high = value.astype(BF16)
            rest = (value - high.astype(F32)).astype(BF16)
            return jnp.concatenate([high, rest], axis=1)

        def pair(j, carry):
            d_s, d_t, d_k = carry
            at = lanes(j)
            dy2 = dybf[:, at].astype(F32)
            x2 = abf[s, :, at].astype(F32)
            inner = x2 * dx0[:, at]
            outer = dy2 * y0[s, :, at] - inner
            lane = iota((2 * 128, HEADS), 0)
            lane = jnp.where(lane >= 128, lane - 128, lane)
            head = 2 * j + jnp.where(lane >= 64, 1, 0)
            pick = (head == iota((2 * 128, HEADS), 1)).astype(BF16)
            skip = jnp.broadcast_to(jnp.sum(dy2 * x2, axis=0, keepdims=True), (8, 128))
            return (
                d_s + dot(two(outer), pick, NN),
                d_t + dot(two(inner), pick, NN),
                d_k + dot(two(skip), pick, NN),
            )

        zero = jnp.zeros((L, HEADS), F32)
        d_s, d_t, d_k = lax.fori_loop(0, PAIRS, pair, (zero, zero, jnp.zeros((8, HEADS), F32)))
        later = dot((iota((L, L), 0) <= iota((L, L), 1)).astype(F32), d_s, NN, HIGH)
        dt = dtc[s]
        z = dtr_ref[s] + db_ref[...]
        g_al = jnp.sum(later * dt, axis=0, keepdims=True) * rate
        g_db = jnp.sum((d_t / dt + later * rate) / (1.0 + jnp.exp(-z)), axis=0, keepdims=True)
        small = (g_al, g_db, d_k[0:1])

        def conv(j):
            at = lanes(j)
            dc = dcpad[0:L, at]
            rows = []
            for k in range(4):
                rows.append(jnp.sum(dc * upad[s, TOP - 3 + k : TOP - 3 + k + L, at], axis=0, keepdims=True))
            rows.append(jnp.sum(dc, axis=0, keepdims=True))
            rows.append(jnp.zeros((3, 128), F32))
            value = jnp.concatenate(rows, axis=0)
            pg[:, at] = value if s == 0 else pg[:, at] + value

        loop(C // 128, conv)
        for i in range(3):
            if s == 0:
                pg[5 + i : 6 + i, 0:HEADS] = small[i]
            else:
                pg[5 + i : 6 + i, 0:HEADS] += small[i]

    def pg_copy(i):
        return remote(pg, pgr.at[d], pg_s.at[i - 1], pg_r.at[i - 1], replica(i))

    def pg_arrival(i):
        src = lax.rem(d + DP - i, DP)
        return remote(pg, pgr.at[src], pg_s.at[i - 1], pg_r.at[i - 1], replica(i))

    def projection():
        for s in range(S):
            for i in range(1, DP):
                yb_arrival(s, i).wait_recv()
                gx_arrival(s, i).wait_recv()

        for q in range(2):

            def block(j):
                rows = yb[:, :, :, lanes(j, 256)].reshape(DP * S * L, 256)
                cols = gcols[:, :, q].reshape(DP * S * L, W)
                win[lanes(j, 256), q * W : (q + 1) * W] = dot(rows, cols, TN).astype(BF16)

            loop(X // 256, block)
        local(win.at[pl.ds(0, X), pl.ds(0, X)], gow_out, 3).start()

    dcpad[L : L + TOP, :] = jnp.zeros((TOP, C), F32)
    grad_mix(0)
    pull(0)
    scatter(0)
    parameters(0)

    @pl.when(p < 3)
    def _():
        reduce(0)

    grad_mix(1)
    pull(1)

    @pl.when(first)
    def _():
        reduce(0)

    scatter(1)
    parameters(1)
    pgr[d] = pg[...]
    for i in range(1, DP):
        pg_copy(i).start()

    @pl.when(last)
    def _():
        projection()

    reduce(1)

    @pl.when(p > 0)
    def _():
        projection()

    for i in range(1, DP):
        pg_arrival(i).wait_recv()
    total = pgr[0]
    for i in range(1, DP):
        total = total + pgr[i]
    pgsum[...] = total
    local(pgsum, pg_out, 4).start()
    for s in range(S):
        for i in range(1, T):
            ox_arrival(s, i).wait_recv()
        for k in range(T):
            gi_v[s, :, k * W : (k + 1) * W] = girecv[s, k]
    local(gi_v, gi_out, 5).start()

    @pl.when(first)
    def _():
        for s in range(S):
            for i in range(1, T):
                cot_copy(s, i).wait_send()

    @pl.when(p > 0)
    def _():
        for s in range(S):
            for i in range(T):
                g_copy(s, i).wait_send()

    for s in range(S):
        for i in range(1, T):
            ox_copy(s, i).wait_send()
        for i in range(1, DP):
            yb_copy(s, i).wait_send()
            gx_copy(s, i).wait_send()
    for i in range(1, DP):
        pg_copy(i).wait_send()
    local(win.at[pl.ds(0, X), pl.ds(0, X)], gow_out, 3).wait()
    local(pgsum, pg_out, 4).wait()
    local(gi_v, gi_out, 5).wait()


def shards(cot, saved_u, dt_raw, in_weight, out_weight, conv_weight, conv_bias, a_log, dt_bias, d_skip):
    any_spec = pl.BlockSpec(memory_space=pl.ANY)
    vmem_spec = pl.BlockSpec(memory_space=pltpu.VMEM)
    sem = pltpu.SemaphoreType.DMA
    scratch = [
        pltpu.VMEM((D, C), BF16),
        pltpu.VMEM((X, D), BF16),
        pltpu.VMEM((S, L, C), BF16),
        pltpu.VMEM((S, L + 2 * TOP, C), F32),
        pltpu.VMEM((S, L, C), F32),
        pltpu.VMEM((S, L, C), BF16),
        pltpu.VMEM((S, PAIRS, 2 * L, 128), BF16),
        pltpu.VMEM((S, PAIRS, 2 * L, L), BF16),
        pltpu.VMEM((S, PAIRS, 2 * L, L), BF16),
        pltpu.VMEM((S, L, X), F32),
        pltpu.VMEM((DP, S, L, X), BF16),
        pltpu.VMEM((HEADS, L), F32),
        pltpu.VMEM((L, HEADS), F32),
        pltpu.VMEM((S, L, HEADS), F32),
        pltpu.VMEM((1, X), F32),
        pltpu.VMEM((S, R, D), BF16),
        pltpu.VMEM((S, T, R, D), BF16),
        pltpu.VMEM((S, T, L, W), BF16),
        pltpu.VMEM((DP, S, 2, L, W), BF16),
        pltpu.VMEM((L, X), F32),
        pltpu.VMEM((L, X), BF16),
        pltpu.VMEM((L, X), F32),
        pltpu.VMEM((L, L), F32),
        pltpu.VMEM((L + TOP, C), F32),
        pltpu.VMEM((L, C), BF16),
        pltpu.VMEM((L, W), F32),
        pltpu.VMEM((T - 1, L, W), BF16),
        pltpu.VMEM((S, T - 1, L, W), BF16),
        pltpu.VMEM((S, L, W), BF16),
        pltpu.VMEM((S, T, R, W), BF16),
        pltpu.VMEM((S, T, R, W), BF16),
        pltpu.VMEM((S, R, D), BF16),
        pltpu.VMEM((8, C), F32),
        pltpu.VMEM((DP, 8, C), F32),
        pltpu.VMEM((8, C), F32),
        sem((6,)),
        sem((S, T - 1)), sem((S, T - 1)),
        sem((S, T)), sem((S, T)),
        sem((S, T - 1)), sem((S, T - 1)),
        sem((S, T - 1)), sem((S, T - 1)),
        sem((S, DP - 1)), sem((S, DP - 1)),
        sem((S, DP - 1)), sem((S, DP - 1)),
        sem((DP - 1,)), sem((DP - 1,)),
    ]
    gi, gow, pg = pl.pallas_call(
        kernel,
        out_shape=(
            jax.ShapeDtypeStruct((S, R, D), BF16),
            jax.ShapeDtypeStruct((X, X), BF16),
            jax.ShapeDtypeStruct((8, C), F32),
        ),
        in_specs=[vmem_spec, any_spec, any_spec, any_spec] + [vmem_spec] * 6,
        out_specs=(any_spec, any_spec, any_spec),
        scratch_shapes=scratch,
        compiler_params=pltpu.CompilerParams(
            collective_id=0, has_side_effects=True, vmem_limit_bytes=64 * 2**20 - 2**16
        ),
        name="mixer_backward",
    )(cot, saved_u[0], in_weight[0], out_weight[0], dt_raw[0], conv_weight[0], conv_bias, a_log, dt_bias, d_skip)
    return (
        gi[None],
        gow[None],
        pg[None, 0:4],
        pg[4:5],
        pg[5:6, :HEADS],
        pg[6:7, :HEADS],
        pg[7:8, :HEADS],
    )


def solution(mesh):
    return jax.shard_map(
        shards,
        mesh=mesh,
        in_specs=(
            P("dp", "tensor", None),
            P("pipe", "dp", None, "tensor"),
            P("pipe", "dp", None, "tensor"),
            P("pipe", None, "tensor"),
            P("pipe", "tensor", None),
            P("pipe", None, "tensor"),
            P("pipe", "tensor"),
            P("pipe", "tensor"),
            P("pipe", "tensor"),
            P("pipe", "tensor"),
        ),
        out_specs=(
            P("pipe", "dp", "tensor", None),
            P("pipe", "tensor", "dp"),
            P("pipe", None, "tensor"),
            P("pipe", "tensor"),
            P("pipe", "tensor"),
            P("pipe", "tensor"),
            P("pipe", "tensor"),
        ),
        check_vma=False,
    )
```

```python
import jax
import jax.numpy as jnp
from jax import lax
from jax.experimental import pallas as pl
from jax.experimental.pallas import tpu as pltpu
from jax.sharding import PartitionSpec as P

F32 = jnp.float32
BF16 = jnp.bfloat16
MESH = pl.DeviceIdType.MESH
NT = (((1,), (1,)), ((), ()))
NN = (((1,), (0,)), ((), ()))
TN = (((0,), (0,)), ((), ()))
HIGH = lax.Precision.HIGHEST

L = 192
D = 4096
X = 1024
C = 1536
HEADS = 16
PAIRS = 8
N = 256
T = 8
Z = 4
Q = 4
B = Z * Q
W = D // B
R = L // T
DP = 4
S = 2
TOP = 8


def dot(a, b, dims, precision=None):
    return lax.dot_general(a, b, dims, preferred_element_type=F32, precision=precision)


def iota(shape, axis):
    return lax.broadcasted_iota(jnp.int32, shape, axis)


def lanes(j, width=128):
    return pl.ds(pl.multiple_of(j * width, width), width)


def loop(count, body):
    def step(i, carry):
        body(i)
        return carry

    lax.fori_loop(0, count, step, 0)


def kernel(
    cot_ref, u_hbm, win_hbm, wout_hbm, dtr_ref, cw_ref, cb_ref, al_ref, db_ref, sk_ref,
    gi_out, gow_out, pg_out,
    win, wout, u_ref, upad, sp, abf, xst, mt, est, y0, yb, sT, scol, dtc, sgc, skl,
    cbuf, crecv, gbuf, gcols, dyacc, dybf, dx0, dcb, dcpad, dubf, own,
    sbuf, rbuf, psum, pbuf, orow, obuf, grecv, gi_v, pg, pgr, pgsum,
    loc, cs_s, cs_r, a_s, a_r, b_s, b_r, c_s, c_r, f_s, f_r, o_s, o_r,
    yb_s, yb_r, gx_s, gx_r, pg_s, pg_r,
):
    p = lax.axis_index("pipe")
    t = lax.axis_index("tensor")
    d = lax.axis_index("dp")
    first = p == 3
    last = p == 0

    def peer(i):
        return (p, lax.rem(t + i, T), d)

    z = t // 2
    side = t % 2
    other = 1 - side

    def above(i):
        return lax.rem(z + i, Z)

    def column(i):
        return (p, 2 * above(i) + side, d)

    def replica(i):
        return (p, t, lax.rem(d + i, DP))

    def local(src, dst, i):
        return pltpu.make_async_copy(src, dst, loc.at[i])

    def remote(src, dst, ssem, rsem, to):
        return pltpu.make_async_remote_copy(
            src_ref=src, dst_ref=dst, send_sem=ssem, recv_sem=rsem, device_id=to, device_id_type=MESH
        )

    local(u_hbm, u_ref, 0).start()
    local(wout_hbm, wout, 1).start()
    local(win_hbm, win, 2).start()

    barrier = pltpu.get_barrier_semaphore()
    for i in range(1, T):
        pl.semaphore_signal(barrier, inc=1, device_id=peer(i), device_id_type=MESH)
    for i in range(1, DP):
        pl.semaphore_signal(barrier, inc=1, device_id=replica(i), device_id_type=MESH)

    @pl.when(p > 0)
    def _():
        for i in range(2):
            pl.semaphore_signal(barrier, inc=1, device_id=(p - 1, 2 * z + i, d), device_id_type=MESH)

    @pl.when(p < 3)
    def _():
        for i in range(2):
            pl.semaphore_signal(barrier, inc=1, device_id=(p + 1, 2 * z + i, d), device_id_type=MESH)

    middle = jnp.logical_and(p > 0, p < 3)

    @pl.when(middle)
    def _():
        pl.semaphore_wait(barrier, T - 1 + DP - 1 + 4)

    @pl.when(jnp.logical_not(middle))
    def _():
        pl.semaphore_wait(barrier, T - 1 + DP - 1 + 2)

    def cot_copy(s, i):
        return remote(cbuf.at[s], crecv.at[s, t], cs_s.at[s, i - 1], cs_r.at[s, i - 1], peer(i))

    def cot_arrival(s, i):
        src = lax.rem(t + T - i, T)
        return remote(cbuf.at[s], crecv.at[s, src], cs_s.at[s, i - 1], cs_r.at[s, i - 1], peer(i))

    def cot_send(s):
        @pl.when(first)
        def _():
            cbuf[s] = cot_ref[s]
            for i in range(1, T):
                cot_copy(s, i).start()
            crecv[s, t] = cot_ref[s]

    cot_send(0)

    rr = iota((L, L), 0)
    tt = iota((L, L), 1)
    upper = (rr <= tt).astype(F32)
    eye = (iota((HEADS, HEADS), 0) == iota((HEADS, HEADS), 1)).astype(F32)

    def upright(row):
        return jnp.sum(eye * row, axis=1, keepdims=True)

    rate = -jnp.exp(al_ref[...])
    spread = (iota((HEADS, X), 0) == iota((HEADS, X), 1) // 64).astype(F32)
    skl[...] = dot(sk_ref[...], spread, NN, HIGH)

    def forward(s):
        upad[s, 0:TOP, :] = jnp.zeros((TOP, C), F32)

        def conv(j):
            at = lanes(j)
            upad[s, TOP : TOP + L, at] = u_ref[s, :, at].astype(F32)
            c = jnp.broadcast_to(cb_ref[:, at], (L, 128))
            for k in range(4):
                c = c + cw_ref[k : k + 1, at] * upad[s, TOP - 3 + k : TOP - 3 + k + L, at]
            sig = 1.0 / (1.0 + jnp.exp(-c))
            sp[s, :, at] = sig * (1.0 + c * (1.0 - sig))
            abf[s, :, at] = (c * sig).astype(BF16)

        loop(C // 128, conv)
        raw = dtr_ref[s] + upright(db_ref[...])
        dt = jnp.maximum(raw, 0.0) + jnp.log1p(jnp.exp(-jnp.abs(raw)))
        total = dot(dt * upright(rate), upper, NN, HIGH)
        sT[...] = total
        scol[...] = dot(total, eye, TN, HIGH)
        dtc[s] = dot(dt, eye, TN, HIGH)
        sgc[s] = dot(1.0 / (1.0 + jnp.exp(-raw)), eye, TN, HIGH)
        dcb[...] = dot(abf[s, :, X : X + N], abf[s, :, X + N : X + 2 * N], NT)

        def pair(j):
            at = lanes(j)
            x2 = abf[s, :, at].astype(F32)
            even = iota((L, 128), 1) < 64
            xst[s, j, 0:L, :] = jnp.where(even, x2, 0.0).astype(BF16)
            xst[s, j, L : 2 * L, :] = jnp.where(even, 0.0, x2).astype(BF16)
            causal = iota((L, L), 1) >= iota((L, L), 0)
            head = iota((L, HEADS), 1)
            for e in range(2):
                h = 2 * j + e
                s_r = jnp.sum(jnp.where(head == h, scol[...], 0.0), axis=1, keepdims=True)
                dt_r = jnp.sum(jnp.where(head == h, dtc[s], 0.0), axis=1, keepdims=True)
                decay = jnp.exp(jnp.minimum(sT[pl.ds(h, 1), :] - s_r, 0.0)) * dt_r
                decay = jnp.where(causal, decay, 0.0)
                est[s, j, e * L : (e + 1) * L, :] = decay.astype(BF16)
                mt[s, j, e * L : (e + 1) * L, :] = (decay * dcb[...]).astype(BF16)
            y2 = dot(mt[s, j], xst[s, j], TN)
            y0[s, :, at] = y2
            yb[d, s, :, at] = (y2 + skl[:, at] * x2).astype(BF16)

        loop(PAIRS, pair)

    def yb_copy(s, i):
        return remote(yb.at[d, s], yb.at[d, s], yb_s.at[s, i - 1], yb_r.at[s, i - 1], replica(i))

    def yb_arrival(s, i):
        src = lax.rem(d + DP - i, DP)
        return remote(yb.at[src, s], yb.at[src, s], yb_s.at[s, i - 1], yb_r.at[s, i - 1], replica(i))

    local(u_hbm, u_ref, 0).wait()
    forward(0)
    cot_send(1)
    forward(1)
    for s in range(S):
        for i in range(1, DP):
            yb_copy(s, i).start()

    local(wout_hbm, wout, 1).wait()

    def b_copy(s, q, to):
        return remote(
            psum.at[s, q], pbuf.at[s, q, side], b_s.at[s, q, to], b_r.at[s, q, side],
            (p - 1, 2 * z + to, d),
        )

    def b_arrival(s, q, src):
        return remote(
            psum.at[s, q], pbuf.at[s, q, src], b_s.at[s, q, src], b_r.at[s, q, src],
            (p + 1, 2 * z + src, d),
        )

    def c_copy(s, q, i):
        at = gbuf.at[s, Q * z + q]
        return remote(at, at, c_s.at[s, q, i - 1], c_r.at[s, q, i - 1], column(i))

    def c_arrival(s, q, i):
        at = gbuf.at[s, Q * above(Z - i) + q]
        return remote(at, at, c_s.at[s, q, i - 1], c_r.at[s, q, i - 1], column(i))

    def gather(s, q):
        @pl.when(p < 3)
        def _():
            for src in range(2):
                b_arrival(s, q, src).wait_recv()

            def block(j):
                at = lanes(j)
                total = pbuf[s, q, 0, :, at].astype(F32) + pbuf[s, q, 1, :, at].astype(F32)
                gbuf[s, Q * z + q, :, at] = total.astype(BF16)

            loop(W // 128, block)
            for i in (2, 1, 3):
                c_copy(s, q, i).start()

    def gx_copy(s, i):
        to = lax.rem(d + i, DP)
        return remote(
            gbuf.at[s, pl.ds(Q * to, Q)], gcols.at[d, s], gx_s.at[s, i - 1], gx_r.at[s, i - 1], replica(i)
        )

    def gx_arrival(s, i):
        src = lax.rem(d + DP - i, DP)
        return remote(
            gbuf.at[s, pl.ds(0, Q)], gcols.at[src, s], gx_s.at[s, i - 1], gx_r.at[s, i - 1], replica(i)
        )

    def grad_mix(s):
        @pl.when(first)
        def _():
            for i in range(1, T):
                cot_arrival(s, i).wait_recv()

            def block(k):
                rows = crecv[s, :, :, lanes(k, W)].astype(F32)
                gbuf[s, k] = rows.reshape(L, W).astype(BF16)

            loop(B, block)

        for q in range(Q):

            @pl.when(p < 3)
            def _():
                for i in range(1, Z):
                    c_arrival(s, q, i).wait_recv()

            part = None
            for i in range(Z):
                k = Q * above(Z - i) + q
                term = dot(gbuf[s, k], wout[:, lanes(k, W)], NT)
                part = term if part is None else part + term
            if q == 0:
                dyacc[...] = part
            elif q < Q - 1:
                dyacc[...] += part
            else:
                dybf[...] = (dyacc[...] + part).astype(BF16)
        for i in range(1, DP):
            gx_copy(s, i).start()
        gcols[d, s] = gbuf[s, pl.ds(Q * d, Q)]

    def o_copy(s):
        return remote(orow.at[s], gi_v.at[s], o_s.at[s], o_r.at[s], (p + 1, t, d))

    def share(s):
        @pl.when(p < 3)
        def _():
            for k in range(B):
                rows = gbuf[s, k].astype(F32).reshape(T, R, W)
                mine = jnp.where(t == 0, rows[0], 0.0)
                for i in range(1, T):
                    mine = jnp.where(t == i, rows[i], mine)
                orow[s, :, k * W : (k + 1) * W] = mine.astype(BF16)
            o_copy(s).start()

    def pull(s):
        dcb[...] = jnp.zeros_like(dcb)

        def pair(j):
            at = lanes(j)
            dy2 = dybf[:, at]
            dm = dot(xst[s, j], dy2, NT)
            dcb[...] += dm[:L] * est[s, j, 0:L, :].astype(F32) + dm[L:] * est[s, j, L : 2 * L, :].astype(F32)
            dx = dot(mt[s, j], dy2, NN)
            dx = jnp.where(iota((L, 128), 1) < 64, dx[:L], dx[L:])
            dx0[:, at] = dx
            dcpad[0:L, at] = (dx + skl[:, at] * dy2.astype(F32)) * sp[s, :, at]

        loop(PAIRS, pair)
        low = dcb[...].astype(BF16)
        dcpad[0:L, X : X + N] = dot(low, abf[s, :, X + N : X + 2 * N], NN) * sp[s, :, X : X + N]
        dcpad[0:L, X + N : X + 2 * N] = (
            dot(low, abf[s, :, X : X + N], TN) * sp[s, :, X + N : X + 2 * N]
        )

        def conv(j):
            at = lanes(j)
            du = cw_ref[3:4, at] * dcpad[0:L, at]
            for k in range(3):
                du = du + cw_ref[k : k + 1, at] * dcpad[3 - k : 3 - k + L, at]
            dubf[:, at] = du.astype(BF16)

        loop(C // 128, conv)

    def a_copy(s, q, i):
        return remote(sbuf.at[q, i - 1], rbuf.at[s, q, i - 1], a_s.at[s, q, i - 1], a_r.at[s, q, i - 1], column(i))

    def scatter(s):
        for q in range(Q):
            for i in (2, 1, 3, 0):
                part = dot(dubf[...], win[lanes(Q * above(i) + q, W), :], NT)
                if i:
                    sbuf[q, i - 1] = part.astype(BF16)
                    a_copy(s, q, i).start()
                else:
                    own[q] = part

    def f_copy(s, i):
        return remote(obuf.at[s, lax.rem(t + i, T)], grecv.at[s, t], f_s.at[s, i - 1], f_r.at[s, i - 1], peer(i))

    def f_arrival(s, i):
        at = grecv.at[s, lax.rem(t + T - i, T)]
        return remote(obuf.at[s, t], at, f_s.at[s, i - 1], f_r.at[s, i - 1], peer(i))

    def combine(s, q):
        for i in range(1, Z):
            a_copy(s, q, i).wait_recv()

        for j in range(W // 128):
            at = slice(j * 128, (j + 1) * 128)
            mine = side == q // (Q // 2)
            total = own[q, :, at] + jnp.where(mine, gbuf[s, Q * z + q, :, at].astype(F32), 0.0)
            for i in range(Z - 1):
                total = total + rbuf[s, q, i, :, at].astype(F32)
            psum[s, q, :, at] = total.astype(BF16)

            @pl.when(last)
            def _():
                obuf[s, :, q, :, at] = total.reshape(T, R, 128).astype(BF16)

        @pl.when(p > 0)
        def _():
            for to in range(2):
                b_copy(s, q, to).start()

        for i in range(1, Z):
            a_copy(s, q, i).wait_send()

    def rows_out(s):
        for i in range(1, T):
            f_copy(s, i).start()
        grecv[s, t] = obuf[s, t]

    def parameters(s):
        def two(value):
            high = value.astype(BF16)
            rest = (value - high.astype(F32)).astype(BF16)
            return jnp.concatenate([high, rest], axis=1)

        def pair(j, carry):
            d_s, d_t, d_k = carry
            at = lanes(j)
            dy2 = dybf[:, at].astype(F32)
            x2 = abf[s, :, at].astype(F32)
            inner = x2 * dx0[:, at]
            outer = dy2 * y0[s, :, at] - inner
            lane = iota((2 * 128, HEADS), 0)
            lane = jnp.where(lane >= 128, lane - 128, lane)
            head = 2 * j + jnp.where(lane >= 64, 1, 0)
            pick = (head == iota((2 * 128, HEADS), 1)).astype(BF16)
            skip = jnp.broadcast_to(jnp.sum(dy2 * x2, axis=0, keepdims=True), (8, 128))
            return (
                d_s + dot(two(outer), pick, NN),
                d_t + dot(two(inner), pick, NN),
                d_k + dot(two(skip), pick, NN),
            )

        zero = jnp.zeros((L, HEADS), F32)
        d_s, d_t, d_k = lax.fori_loop(0, PAIRS, pair, (zero, zero, jnp.zeros((8, HEADS), F32)))
        later = dot((iota((L, L), 0) <= iota((L, L), 1)).astype(F32), d_s, NN, HIGH)
        dt = dtc[s]
        g_al = jnp.sum(later * dt, axis=0, keepdims=True) * rate
        g_db = jnp.sum((d_t / dt + later * rate) * sgc[s], axis=0, keepdims=True)
        small = (g_al, g_db, d_k[0:1])

        def conv(j):
            at = lanes(j)
            dc = dcpad[0:L, at]
            rows = []
            for k in range(4):
                rows.append(jnp.sum(dc * upad[s, TOP - 3 + k : TOP - 3 + k + L, at], axis=0, keepdims=True))
            rows.append(jnp.sum(dc, axis=0, keepdims=True))
            rows.append(jnp.zeros((3, 128), F32))
            value = jnp.concatenate(rows, axis=0)
            pg[:, at] = value if s == 0 else pg[:, at] + value

        loop(C // 128, conv)
        for i in range(3):
            if s == 0:
                pg[5 + i : 6 + i, 0:HEADS] = small[i]
            else:
                pg[5 + i : 6 + i, 0:HEADS] += small[i]

    def pg_copy(i):
        return remote(pg, pgr.at[d], pg_s.at[i - 1], pg_r.at[i - 1], replica(i))

    def pg_arrival(i):
        src = lax.rem(d + DP - i, DP)
        return remote(pg, pgr.at[src], pg_s.at[i - 1], pg_r.at[i - 1], replica(i))

    def projection():
        for s in range(S):
            for i in range(1, DP):
                yb_arrival(s, i).wait_recv()
                gx_arrival(s, i).wait_recv()

        for k in range(2):

            def block(j):
                rows = yb[:, :, :, lanes(j, 256)].reshape(DP * S * L, 256)
                cols = jnp.concatenate(
                    [gcols[:, :, 2 * k + e].reshape(DP * S * L, W) for e in range(2)], axis=1
                )
                win[lanes(j, 256), 2 * k * W : 2 * (k + 1) * W] = dot(rows, cols, TN).astype(BF16)

            loop(X // 256, block)
        local(win.at[pl.ds(0, X), pl.ds(0, X)], gow_out, 3).start()

    dcpad[L : L + TOP, :] = jnp.zeros((TOP, C), F32)
    for q in range(Q):
        gather(0, q)
    grad_mix(0)
    pull(0)
    local(win_hbm, win, 2).wait()
    scatter(0)
    share(0)
    parameters(0)
    for q in range(Q):
        combine(0, q)

    @pl.when(last)
    def _():
        rows_out(0)

    for q in range(Q):
        gather(1, q)
    grad_mix(1)
    pull(1)
    scatter(1)
    share(1)
    parameters(1)
    pgr[d] = pg[...]
    for i in range(1, DP):
        pg_copy(i).start()
    for q in range(Q):
        combine(1, q)

    @pl.when(last)
    def _():
        rows_out(1)

    projection()

    for i in range(1, DP):
        pg_arrival(i).wait_recv()
    total = pgr[0]
    for i in range(1, DP):
        total = total + pgr[i]
    pgsum[...] = total
    local(pgsum, pg_out, 4).start()

    @pl.when(last)
    def _():
        for s in range(S):
            for i in range(1, T):
                f_arrival(s, i).wait_recv()
            for k in range(B):
                a, b = grecv[s, 2 * (k // Q), k % Q], grecv[s, 2 * (k // Q) + 1, k % Q]
                gi_v[s, :, k * W : (k + 1) * W] = (a.astype(F32) + b.astype(F32)).astype(BF16)

    @pl.when(p > 0)
    def _():
        for s in range(S):
            remote(orow.at[s], gi_v.at[s], o_s.at[s], o_r.at[s], (p - 1, t, d)).wait_recv()

    local(gi_v, gi_out, 5).start()

    @pl.when(first)
    def _():
        for s in range(S):
            for i in range(1, T):
                cot_copy(s, i).wait_send()

    @pl.when(p < 3)
    def _():
        for s in range(S):
            o_copy(s).wait_send()
            for q in range(Q):
                for i in range(1, Z):
                    c_copy(s, q, i).wait_send()

    @pl.when(p > 0)
    def _():
        for s in range(S):
            for q in range(Q):
                for to in range(2):
                    b_copy(s, q, to).wait_send()

    @pl.when(last)
    def _():
        for s in range(S):
            for i in range(1, T):
                f_copy(s, i).wait_send()

    for s in range(S):
        for i in range(1, DP):
            yb_copy(s, i).wait_send()
            gx_copy(s, i).wait_send()
    for i in range(1, DP):
        pg_copy(i).wait_send()
    local(win.at[pl.ds(0, X), pl.ds(0, X)], gow_out, 3).wait()
    local(pgsum, pg_out, 4).wait()
    local(gi_v, gi_out, 5).wait()


def finish(gi_ref, gow_ref, pg_ref, gi, gow, cw, cb, al, db, sk):
    gi[...] = gi_ref[...]

    def rows(j):
        gow[lanes(j, 64), :] = gow_ref[lanes(j, 64), :]

    loop(X // 64, rows)
    cw[...] = pg_ref[0:4, :]
    cb[...] = pg_ref[4:5, :]
    al[...] = pg_ref[5:6, 0:HEADS]
    db[...] = pg_ref[6:7, 0:HEADS]
    sk[...] = pg_ref[7:8, 0:HEADS]


def shards(cot, saved_u, dt_raw, in_weight, out_weight, conv_weight, conv_bias, a_log, dt_bias, d_skip):
    any_spec = pl.BlockSpec(memory_space=pl.ANY)
    vmem_spec = pl.BlockSpec(memory_space=pltpu.VMEM)
    sem = pltpu.SemaphoreType.DMA
    scratch = [
        pltpu.VMEM((D, C), BF16),
        pltpu.VMEM((X, D), BF16),
        pltpu.VMEM((S, L, C), BF16),
        pltpu.VMEM((S, L + 2 * TOP, C), F32),
        pltpu.VMEM((S, L, C), F32),
        pltpu.VMEM((S, L, C), BF16),
        pltpu.VMEM((S, PAIRS, 2 * L, 128), BF16),
        pltpu.VMEM((S, PAIRS, 2 * L, L), BF16),
        pltpu.VMEM((S, PAIRS, 2 * L, L), BF16),
        pltpu.VMEM((S, L, X), F32),
        pltpu.VMEM((DP, S, L, X), BF16),
        pltpu.VMEM((HEADS, L), F32),
        pltpu.VMEM((L, HEADS), F32),
        pltpu.VMEM((S, L, HEADS), F32),
        pltpu.VMEM((S, L, HEADS), F32),
        pltpu.VMEM((1, X), F32),
        pltpu.VMEM((S, R, D), BF16),
        pltpu.VMEM((S, T, R, D), BF16),
        pltpu.VMEM((S, B, L, W), BF16),
        pltpu.VMEM((DP, S, Q, L, W), BF16),
        pltpu.VMEM((L, X), F32),
        pltpu.VMEM((L, X), BF16),
        pltpu.VMEM((L, X), F32),
        pltpu.VMEM((L, L), F32),
        pltpu.VMEM((L + TOP, C), F32),
        pltpu.VMEM((L, C), BF16),
        pltpu.VMEM((Q, L, W), F32),
        pltpu.VMEM((Q, Z - 1, L, W), BF16),
        pltpu.VMEM((S, Q, Z - 1, L, W), BF16),
        pltpu.VMEM((S, Q, L, W), BF16),
        pltpu.VMEM((S, Q, 2, L, W), BF16),
        pltpu.VMEM((S, R, D), BF16),
        pltpu.VMEM((S, T, Q, R, W), BF16),
        pltpu.VMEM((S, T, Q, R, W), BF16),
        pltpu.VMEM((S, R, D), BF16),
        pltpu.VMEM((8, C), F32),
        pltpu.VMEM((DP, 8, C), F32),
        pltpu.VMEM((8, C), F32),
        sem((6,)),
        sem((S, T - 1)), sem((S, T - 1)),
        sem((S, Q, Z - 1)), sem((S, Q, Z - 1)),
        sem((S, Q, 2)), sem((S, Q, 2)),
        sem((S, Q, Z - 1)), sem((S, Q, Z - 1)),
        sem((S, T - 1)), sem((S, T - 1)),
        sem((S,)), sem((S,)),
        sem((S, DP - 1)), sem((S, DP - 1)),
        sem((S, DP - 1)), sem((S, DP - 1)),
        sem((DP - 1,)), sem((DP - 1,)),
    ]
    gi, gow, pg = pl.pallas_call(
        kernel,
        out_shape=(
            jax.ShapeDtypeStruct((S, R, D), BF16),
            jax.ShapeDtypeStruct((X, X), BF16),
            jax.ShapeDtypeStruct((8, C), F32),
        ),
        in_specs=[vmem_spec, any_spec, any_spec, any_spec] + [vmem_spec] * 6,
        out_specs=(any_spec, any_spec, any_spec),
        scratch_shapes=scratch,
        compiler_params=pltpu.CompilerParams(
            collective_id=0, has_side_effects=True, vmem_limit_bytes=64 * 2**20 - 2**16
        ),
        name="mixer_backward",
    )(cot, saved_u[0], in_weight[0], out_weight[0], jnp.swapaxes(dt_raw[0], 1, 2), conv_weight[0], conv_bias, a_log, dt_bias, d_skip)
    outs = pl.pallas_call(
        finish,
        out_shape=(
            jax.ShapeDtypeStruct((S, R, D), BF16),
            jax.ShapeDtypeStruct((X, X), BF16),
            jax.ShapeDtypeStruct((4, C), F32),
            jax.ShapeDtypeStruct((1, C), F32),
            jax.ShapeDtypeStruct((1, HEADS), F32),
            jax.ShapeDtypeStruct((1, HEADS), F32),
            jax.ShapeDtypeStruct((1, HEADS), F32),
        ),
        in_specs=[vmem_spec] * 3,
        out_specs=(vmem_spec,) * 7,
        compiler_params=pltpu.CompilerParams(vmem_limit_bytes=16 * 2**20),
        name="finish",
    )(gi, gow, pg)
    gi, gow, cw, cb, al, db, sk = outs
    return gi[None], gow[None], cw[None], cb, al, db, sk


def solution(mesh):
    return jax.shard_map(
        shards,
        mesh=mesh,
        in_specs=(
            P("dp", "tensor", None),
            P("pipe", "dp", None, "tensor"),
            P("pipe", "dp", None, "tensor"),
            P("pipe", None, "tensor"),
            P("pipe", "tensor", None),
            P("pipe", None, "tensor"),
            P("pipe", "tensor"),
            P("pipe", "tensor"),
            P("pipe", "tensor"),
            P("pipe", "tensor"),
        ),
        out_specs=(
            P("pipe", "dp", "tensor", None),
            P("pipe", "tensor", "dp"),
            P("pipe", None, "tensor"),
            P("pipe", "tensor"),
            P("pipe", "tensor"),
            P("pipe", "tensor"),
            P("pipe", "tensor"),
        ),
        check_vma=False,
    )
```

```python
import jax
import jax.numpy as jnp
from jax import lax
from jax.experimental import pallas as pl
from jax.experimental.pallas import tpu as pltpu
from jax.sharding import PartitionSpec as P

F32 = jnp.float32
BF16 = jnp.bfloat16
MESH = pl.DeviceIdType.MESH
NT = (((1,), (1,)), ((), ()))
NN = (((1,), (0,)), ((), ()))
TN = (((0,), (0,)), ((), ()))
HIGH = lax.Precision.HIGHEST

L = 192
D = 4096
X = 1024
C = 1536
HEADS = 16
PAIRS = 8
N = 256
T = 8
Z = 4
Q = 4
B = Z * Q
W = D // B
R = L // T
DP = 4
S = 2
TOP = 8


def dot(a, b, dims, precision=None):
    return lax.dot_general(a, b, dims, preferred_element_type=F32, precision=precision)


def iota(shape, axis):
    return lax.broadcasted_iota(jnp.int32, shape, axis)


def lanes(j, width=128):
    return pl.ds(pl.multiple_of(j * width, width), width)


def loop(count, body):
    def step(i, carry):
        body(i)
        return carry

    lax.fori_loop(0, count, step, 0)


def kernel(
    cot_ref, u_hbm, win_hbm, wout_hbm, dtr_ref, cw_ref, cb_ref, al_ref, db_ref, sk_ref,
    gi_out, gow_out, pg_out,
    win, wout, u_ref, upad, sp, abf, xst, mt, est, y0, yb, sT, scol, dtc, sgc, skl,
    cbuf, crecv, gbuf, gcols, dyacc, dybf, dx0, dcb, dcpad, own,
    sbuf, rbuf, psum, pbuf, orow, obuf, gi_v, pg, pgr, pgsum,
    loc, cs_s, cs_r, a_s, a_r, b_s, b_r, c_s, c_r, f_s, f_r, o_s, o_r,
    yb_s, yb_r, gx_s, gx_r, pg_s, pg_r,
):
    p = lax.axis_index("pipe")
    t = lax.axis_index("tensor")
    d = lax.axis_index("dp")
    first = p == 3
    last = p == 0

    def peer(i):
        return (p, lax.rem(t + i, T), d)

    z = t // 2
    side = t % 2
    other = 1 - side

    def above(i):
        return lax.rem(z + i, Z)

    def column(i):
        return (p, 2 * above(i) + side, d)

    def replica(i):
        return (p, t, lax.rem(d + i, DP))

    def local(src, dst, i):
        return pltpu.make_async_copy(src, dst, loc.at[i])

    def remote(src, dst, ssem, rsem, to):
        return pltpu.make_async_remote_copy(
            src_ref=src, dst_ref=dst, send_sem=ssem, recv_sem=rsem, device_id=to, device_id_type=MESH
        )

    local(u_hbm, u_ref, 0).start()
    local(cot_ref, cbuf, 6).start()
    local(wout_hbm, wout, 1).start()
    local(win_hbm, win, 2).start()

    barrier = pltpu.get_barrier_semaphore()
    for i in range(1, T):
        pl.semaphore_signal(barrier, inc=1, device_id=peer(i), device_id_type=MESH)
    for i in range(1, DP):
        pl.semaphore_signal(barrier, inc=1, device_id=replica(i), device_id_type=MESH)

    @pl.when(p > 0)
    def _():
        for i in range(2):
            pl.semaphore_signal(barrier, inc=1, device_id=(p - 1, 2 * z + i, d), device_id_type=MESH)

    @pl.when(p < 3)
    def _():
        for i in range(2):
            pl.semaphore_signal(barrier, inc=1, device_id=(p + 1, 2 * z + i, d), device_id_type=MESH)

    middle = jnp.logical_and(p > 0, p < 3)

    @pl.when(middle)
    def _():
        pl.semaphore_wait(barrier, T - 1 + DP - 1 + 4)

    @pl.when(jnp.logical_not(middle))
    def _():
        pl.semaphore_wait(barrier, T - 1 + DP - 1 + 2)

    def cot_copy(s, i):
        return remote(cbuf.at[s], crecv.at[s, t], cs_s.at[s, i - 1], cs_r.at[s, i - 1], peer(i))

    def cot_arrival(s, i):
        src = lax.rem(t + T - i, T)
        return remote(cbuf.at[s], crecv.at[s, src], cs_s.at[s, i - 1], cs_r.at[s, i - 1], peer(i))

    def cot_send(s):
        @pl.when(first)
        def _():
            for i in range(1, T):
                cot_copy(s, i).start()
            crecv[s, t] = cbuf[s]

    local(cot_ref, cbuf, 6).wait()
    cot_send(0)

    rr = iota((L, L), 0)
    tt = iota((L, L), 1)
    upper = (rr <= tt).astype(F32)
    eye = (iota((HEADS, HEADS), 0) == iota((HEADS, HEADS), 1)).astype(F32)

    def upright(row):
        return jnp.sum(eye * row, axis=1, keepdims=True)

    rate = -jnp.exp(al_ref[...])
    spread = (iota((HEADS, X), 0) == iota((HEADS, X), 1) // 64).astype(F32)
    skl[...] = dot(sk_ref[...], spread, NN, HIGH)

    def forward(s):
        upad[s, 0:TOP, :] = jnp.zeros((TOP, C), F32)

        def conv(j):
            at = lanes(j)
            upad[s, TOP : TOP + L, at] = u_ref[s, :, at].astype(F32)
            c = jnp.broadcast_to(cb_ref[:, at], (L, 128))
            for k in range(4):
                c = c + cw_ref[k : k + 1, at] * upad[s, TOP - 3 + k : TOP - 3 + k + L, at]
            sig = 1.0 / (1.0 + jnp.exp(-c))
            sp[s, :, at] = sig * (1.0 + c * (1.0 - sig))
            abf[s, :, at] = (c * sig).astype(BF16)

        loop(C // 128, conv)
        raw = dtr_ref[s] + upright(db_ref[...])
        dt = jnp.maximum(raw, 0.0) + jnp.log1p(jnp.exp(-jnp.abs(raw)))
        total = dot(dt * upright(rate), upper, NN, HIGH)
        sT[...] = total
        scol[...] = dot(total, eye, TN, HIGH)
        dtc[s] = dot(dt, eye, TN, HIGH)
        sgc[s] = dot(1.0 / (1.0 + jnp.exp(-raw)), eye, TN, HIGH)
        dcb[...] = dot(abf[s, :, X : X + N], abf[s, :, X + N : X + 2 * N], NT)

        def pair(j):
            at = lanes(j)
            x2 = abf[s, :, at].astype(F32)
            even = iota((L, 128), 1) < 64
            xst[s, j, 0:L, :] = jnp.where(even, x2, 0.0).astype(BF16)
            xst[s, j, L : 2 * L, :] = jnp.where(even, 0.0, x2).astype(BF16)
            causal = iota((L, L), 1) >= iota((L, L), 0)
            head = iota((L, HEADS), 1)
            for e in range(2):
                h = 2 * j + e
                s_r = jnp.sum(jnp.where(head == h, scol[...], 0.0), axis=1, keepdims=True)
                dt_r = jnp.sum(jnp.where(head == h, dtc[s], 0.0), axis=1, keepdims=True)
                decay = jnp.exp(jnp.minimum(sT[pl.ds(h, 1), :] - s_r, 0.0)) * dt_r
                decay = jnp.where(causal, decay, 0.0)
                est[s, j, e * L : (e + 1) * L, :] = decay.astype(BF16)
                mt[s, j, e * L : (e + 1) * L, :] = (decay * dcb[...]).astype(BF16)
            y2 = dot(mt[s, j], xst[s, j], TN)
            y0[s, :, at] = y2
            yb[d, s, :, at] = (y2 + skl[:, at] * x2).astype(BF16)

        loop(PAIRS, pair)

    def yb_copy(s, i):
        return remote(yb.at[d, s], yb.at[d, s], yb_s.at[s, i - 1], yb_r.at[s, i - 1], replica(i))

    def yb_arrival(s, i):
        src = lax.rem(d + DP - i, DP)
        return remote(yb.at[src, s], yb.at[src, s], yb_s.at[s, i - 1], yb_r.at[s, i - 1], replica(i))

    local(u_hbm, u_ref, 0).wait()
    forward(0)
    cot_send(1)
    forward(1)
    for s in range(S):
        for i in range(1, DP):
            yb_copy(s, i).start()

    local(wout_hbm, wout, 1).wait()

    def b_copy(s, q, to):
        return remote(
            psum.at[s, q], pbuf.at[s, q, side], b_s.at[s, q, to], b_r.at[s, q, side],
            (p - 1, 2 * z + to, d),
        )

    def b_arrival(s, q, src):
        return remote(
            psum.at[s, q], pbuf.at[s, q, src], b_s.at[s, q, src], b_r.at[s, q, src],
            (p + 1, 2 * z + src, d),
        )

    def c_copy(s, q, i):
        at = gbuf.at[s, Q * z + q]
        return remote(at, at, c_s.at[s, q, i - 1], c_r.at[s, q, i - 1], column(i))

    def c_arrival(s, q, i):
        at = gbuf.at[s, Q * above(Z - i) + q]
        return remote(at, at, c_s.at[s, q, i - 1], c_r.at[s, q, i - 1], column(i))

    def gather(s, q):
        @pl.when(p < 3)
        def _():
            for src in range(2):
                b_arrival(s, q, src).wait_recv()

            def block(j):
                at = lanes(j)
                total = pbuf[s, q, 0, :, at].astype(F32) + pbuf[s, q, 1, :, at].astype(F32)
                gbuf[s, Q * z + q, :, at] = total.astype(BF16)

            loop(W // 128, block)
            for i in (2, 1, 3):
                c_copy(s, q, i).start()

    def gx_copy(s, i):
        to = lax.rem(d + i, DP)
        return remote(
            gbuf.at[s, pl.ds(Q * to, Q)], gcols.at[d, s], gx_s.at[s, i - 1], gx_r.at[s, i - 1], replica(i)
        )

    def gx_arrival(s, i):
        src = lax.rem(d + DP - i, DP)
        return remote(
            gbuf.at[s, pl.ds(0, Q)], gcols.at[src, s], gx_s.at[s, i - 1], gx_r.at[s, i - 1], replica(i)
        )

    def grad_mix(s):
        @pl.when(first)
        def _():
            for i in range(1, T):
                cot_arrival(s, i).wait_recv()

            def block(k):
                rows = crecv[s, :, :, lanes(k, W)].astype(F32)
                gbuf[s, k] = rows.reshape(L, W).astype(BF16)

            loop(B, block)

        for q in range(Q):

            @pl.when(p < 3)
            def _():
                for i in range(1, Z):
                    c_arrival(s, q, i).wait_recv()

            part = None
            for i in range(Z):
                k = Q * above(Z - i) + q
                term = dot(gbuf[s, k], wout[:, lanes(k, W)], NT)
                part = term if part is None else part + term
            if q == 0:
                dyacc[...] = part
            elif q < Q - 1:
                dyacc[...] += part
            else:
                dybf[s] = (dyacc[...] + part).astype(BF16)
        for i in range(1, DP):
            gx_copy(s, i).start()
        gcols[d, s] = gbuf[s, pl.ds(Q * d, Q)]

    def o_copy(s):
        return remote(orow.at[s], gi_v.at[s], o_s.at[s], o_r.at[s], (p + 1, t, d))

    def share(s):
        @pl.when(p < 3)
        def _():
            for k in range(B):
                rows = gbuf[s, k].astype(F32).reshape(T, R, W)
                mine = jnp.where(t == 0, rows[0], 0.0)
                for i in range(1, T):
                    mine = jnp.where(t == i, rows[i], mine)
                orow[s, :, k * W : (k + 1) * W] = mine.astype(BF16)
            o_copy(s).start()

    def pull(s):
        dcb[...] = jnp.zeros_like(dcb)

        def pair(j):
            at = lanes(j)
            dy2 = dybf[s, :, at]
            dm = dot(xst[s, j], dy2, NT)
            dcb[...] += dm[:L] * est[s, j, 0:L, :].astype(F32) + dm[L:] * est[s, j, L : 2 * L, :].astype(F32)
            dx = dot(mt[s, j], dy2, NN)
            dx = jnp.where(iota((L, 128), 1) < 64, dx[:L], dx[L:])
            dx0[s, :, at] = dx
            dcpad[s, 0:L, at] = (dx + skl[:, at] * dy2.astype(F32)) * sp[s, :, at]

        loop(PAIRS, pair)
        low = dcb[...].astype(BF16)
        dcpad[s, 0:L, X : X + N] = dot(low, abf[s, :, X + N : X + 2 * N], NN) * sp[s, :, X : X + N]
        dcpad[s, 0:L, X + N : X + 2 * N] = (
            dot(low, abf[s, :, X : X + N], TN) * sp[s, :, X + N : X + 2 * N]
        )

        def conv(j):
            at = lanes(j)
            du = cw_ref[3:4, at] * dcpad[s, 0:L, at]
            for k in range(3):
                du = du + cw_ref[k : k + 1, at] * dcpad[s, 3 - k : 3 - k + L, at]
            u_ref[0, :, at] = du.astype(BF16)

        loop(C // 128, conv)

    def a_copy(s, q, i):
        return remote(sbuf.at[q, i - 1], rbuf.at[s, q, i - 1], a_s.at[s, q, i - 1], a_r.at[s, q, i - 1], column(i))

    def scatter(s):
        for q in range(Q):
            for i in (2, 1, 3, 0):
                part = dot(u_ref[0], win[lanes(Q * above(i) + q, W), :], NT)
                if i:
                    sbuf[q, i - 1] = part.astype(BF16)
                    a_copy(s, q, i).start()
                else:
                    own[q] = part

    def f_copy(s, i):
        return remote(obuf.at[s, lax.rem(t + i, T)], crecv.at[s, t, :, pl.ds(0, Q * W)], f_s.at[s, i - 1], f_r.at[s, i - 1], peer(i))

    def f_arrival(s, i):
        at = crecv.at[s, lax.rem(t + T - i, T), :, pl.ds(0, Q * W)]
        return remote(obuf.at[s, t], at, f_s.at[s, i - 1], f_r.at[s, i - 1], peer(i))

    def combine(s, q):
        for i in range(1, Z):
            a_copy(s, q, i).wait_recv()

        for j in range(W // 128):
            at = slice(j * 128, (j + 1) * 128)
            mine = side == q // (Q // 2)
            total = own[q, :, at] + jnp.where(mine, gbuf[s, Q * z + q, :, at].astype(F32), 0.0)
            for i in range(Z - 1):
                total = total + rbuf[s, q, i, :, at].astype(F32)
            psum[s, q, :, at] = total.astype(BF16)

            @pl.when(last)
            def _():
                obuf[s, :, :, q * W + j * 128 : q * W + (j + 1) * 128] = total.reshape(T, R, 128).astype(BF16)

        @pl.when(p > 0)
        def _():
            for to in range(2):
                b_copy(s, q, to).start()

        for i in range(1, Z):
            a_copy(s, q, i).wait_send()

    def rows_out(s):
        for i in range(1, T):
            f_copy(s, i).start()
        crecv[s, t, :, 0 : Q * W] = obuf[s, t]

    def parameters(s):
        def two(value):
            high = value.astype(BF16)
            rest = (value - high.astype(F32)).astype(BF16)
            return jnp.concatenate([high, rest], axis=1)

        def pair(j, carry):
            d_s, d_t, d_k = carry
            at = lanes(j)
            dy2 = dybf[s, :, at].astype(F32)
            x2 = abf[s, :, at].astype(F32)
            inner = x2 * dx0[s, :, at]
            outer = dy2 * y0[s, :, at] - inner
            lane = iota((2 * 128, HEADS), 0)
            lane = jnp.where(lane >= 128, lane - 128, lane)
            head = 2 * j + jnp.where(lane >= 64, 1, 0)
            pick = (head == iota((2 * 128, HEADS), 1)).astype(BF16)
            skip = jnp.broadcast_to(jnp.sum(dy2 * x2, axis=0, keepdims=True), (8, 128))
            return (
                d_s + dot(two(outer), pick, NN),
                d_t + dot(two(inner), pick, NN),
                d_k + dot(two(skip), pick, NN),
            )

        zero = jnp.zeros((L, HEADS), F32)
        d_s, d_t, d_k = lax.fori_loop(0, PAIRS, pair, (zero, zero, jnp.zeros((8, HEADS), F32)))
        later = dot((iota((L, L), 0) <= iota((L, L), 1)).astype(F32), d_s, NN, HIGH)
        dt = dtc[s]
        g_al = jnp.sum(later * dt, axis=0, keepdims=True) * rate
        g_db = jnp.sum((d_t / dt + later * rate) * sgc[s], axis=0, keepdims=True)
        small = (g_al, g_db, d_k[0:1])

        def conv(j):
            at = lanes(j)
            dc = dcpad[s, 0:L, at]
            rows = []
            for k in range(4):
                rows.append(jnp.sum(dc * upad[s, TOP - 3 + k : TOP - 3 + k + L, at], axis=0, keepdims=True))
            rows.append(jnp.sum(dc, axis=0, keepdims=True))
            rows.append(jnp.zeros((3, 128), F32))
            value = jnp.concatenate(rows, axis=0)
            pg[:, at] = value if s == 0 else pg[:, at] + value

        loop(C // 128, conv)
        for i in range(3):
            if s == 0:
                pg[5 + i : 6 + i, 0:HEADS] = small[i]
            else:
                pg[5 + i : 6 + i, 0:HEADS] += small[i]

    def pg_copy(i):
        return remote(pg, pgr.at[d], pg_s.at[i - 1], pg_r.at[i - 1], replica(i))

    def pg_arrival(i):
        src = lax.rem(d + DP - i, DP)
        return remote(pg, pgr.at[src], pg_s.at[i - 1], pg_r.at[i - 1], replica(i))

    def projection():
        for s in range(S):
            for i in range(1, DP):
                yb_arrival(s, i).wait_recv()
                gx_arrival(s, i).wait_recv()

        for k in range(2):

            def block(j):
                rows = yb[:, :, :, lanes(j, 256)].reshape(DP * S * L, 256)
                cols = jnp.concatenate(
                    [gcols[:, :, 2 * k + e].reshape(DP * S * L, W) for e in range(2)], axis=1
                )
                win[lanes(j, 256), 2 * k * W : 2 * (k + 1) * W] = dot(rows, cols, TN).astype(BF16)

            loop(X // 256, block)
        local(win.at[pl.ds(0, X), pl.ds(0, X)], gow_out, 3).start()

    dcpad[:, L : L + TOP, :] = jnp.zeros((S, TOP, C), F32)
    for q in range(Q):
        gather(0, q)
    grad_mix(0)
    pull(0)
    local(win_hbm, win, 2).wait()
    scatter(0)
    for q in range(Q):
        gather(1, q)
    for q in range(Q):
        combine(0, q)

    @pl.when(last)
    def _():
        rows_out(0)


    @pl.when(p < 3)
    def _():
        share(0)
        parameters(0)

    grad_mix(1)
    pull(1)
    scatter(1)

    @pl.when(first)
    def _():
        parameters(0)

    for q in range(Q):
        combine(1, q)

    @pl.when(last)
    def _():
        rows_out(1)

    share(1)
    parameters(1)
    pgr[d] = pg[...]
    for i in range(1, DP):
        pg_copy(i).start()
    projection()

    for i in range(1, DP):
        pg_arrival(i).wait_recv()
    total = pgr[0]
    for i in range(1, DP):
        total = total + pgr[i]
    pgsum[...] = total
    local(pgsum, pg_out, 4).start()

    @pl.when(last)
    def _():
        for s in range(S):
            for i in range(1, T):
                f_arrival(s, i).wait_recv()
            for k in range(Z):
                a, b = crecv[s, 2 * k, :, 0 : Q * W], crecv[s, 2 * k + 1, :, 0 : Q * W]
                gi_v[s, :, k * Q * W : (k + 1) * Q * W] = (a.astype(F32) + b.astype(F32)).astype(BF16)

    @pl.when(p > 0)
    def _():
        for s in range(S):
            remote(orow.at[s], gi_v.at[s], o_s.at[s], o_r.at[s], (p - 1, t, d)).wait_recv()

    local(gi_v, gi_out, 5).start()

    @pl.when(first)
    def _():
        for s in range(S):
            for i in range(1, T):
                cot_copy(s, i).wait_send()

    @pl.when(p < 3)
    def _():
        for s in range(S):
            o_copy(s).wait_send()
            for q in range(Q):
                for i in range(1, Z):
                    c_copy(s, q, i).wait_send()

    @pl.when(p > 0)
    def _():
        for s in range(S):
            for q in range(Q):
                for to in range(2):
                    b_copy(s, q, to).wait_send()

    @pl.when(last)
    def _():
        for s in range(S):
            for i in range(1, T):
                f_copy(s, i).wait_send()

    for s in range(S):
        for i in range(1, DP):
            yb_copy(s, i).wait_send()
            gx_copy(s, i).wait_send()
    for i in range(1, DP):
        pg_copy(i).wait_send()
    local(win.at[pl.ds(0, X), pl.ds(0, X)], gow_out, 3).wait()
    local(pgsum, pg_out, 4).wait()
    local(gi_v, gi_out, 5).wait()


def finish(gi_ref, gow_ref, pg_ref, gi, gow, cw, cb, al, db, sk, pg, sems):
    copies = [
        pltpu.make_async_copy(src, dst, sems.at[i])
        for i, (src, dst) in enumerate(((gow_ref, gow), (gi_ref, gi), (pg_ref, pg)))
    ]
    for copy in copies:
        copy.start()
    copies[2].wait()
    cw[...] = pg[0:4, :]
    cb[...] = pg[4:5, :]
    al[...] = pg[5:6, 0:HEADS]
    db[...] = pg[6:7, 0:HEADS]
    sk[...] = pg[7:8, 0:HEADS]
    copies[1].wait()
    copies[0].wait()


def shards(cot, saved_u, dt_raw, in_weight, out_weight, conv_weight, conv_bias, a_log, dt_bias, d_skip):
    any_spec = pl.BlockSpec(memory_space=pl.ANY)
    vmem_spec = pl.BlockSpec(memory_space=pltpu.VMEM)
    sem = pltpu.SemaphoreType.DMA
    scratch = [
        pltpu.VMEM((D, C), BF16),
        pltpu.VMEM((X, D), BF16),
        pltpu.VMEM((S, L, C), BF16),
        pltpu.VMEM((S, L + 2 * TOP, C), F32),
        pltpu.VMEM((S, L, C), F32),
        pltpu.VMEM((S, L, C), BF16),
        pltpu.VMEM((S, PAIRS, 2 * L, 128), BF16),
        pltpu.VMEM((S, PAIRS, 2 * L, L), BF16),
        pltpu.VMEM((S, PAIRS, 2 * L, L), BF16),
        pltpu.VMEM((S, L, X), F32),
        pltpu.VMEM((DP, S, L, X), BF16),
        pltpu.VMEM((HEADS, L), F32),
        pltpu.VMEM((L, HEADS), F32),
        pltpu.VMEM((S, L, HEADS), F32),
        pltpu.VMEM((S, L, HEADS), F32),
        pltpu.VMEM((1, X), F32),
        pltpu.VMEM((S, R, D), BF16),
        pltpu.VMEM((S, T, R, D), BF16),
        pltpu.VMEM((S, B, L, W), BF16),
        pltpu.VMEM((DP, S, Q, L, W), BF16),
        pltpu.VMEM((L, X), F32),
        pltpu.VMEM((S, L, X), BF16),
        pltpu.VMEM((S, L, X), F32),
        pltpu.VMEM((L, L), F32),
        pltpu.VMEM((S, L + TOP, C), F32),
        pltpu.VMEM((Q, L, W), F32),
        pltpu.VMEM((Q, Z - 1, L, W), BF16),
        pltpu.VMEM((S, Q, Z - 1, L, W), BF16),
        pltpu.VMEM((S, Q, L, W), BF16),
        pltpu.VMEM((S, Q, 2, L, W), BF16),
        pltpu.VMEM((S, R, D), BF16),
        pltpu.VMEM((S, T, R, Q * W), BF16),
        pltpu.VMEM((S, R, D), BF16),
        pltpu.VMEM((8, C), F32),
        pltpu.VMEM((DP, 8, C), F32),
        pltpu.VMEM((8, C), F32),
        sem((7,)),
        sem((S, T - 1)), sem((S, T - 1)),
        sem((S, Q, Z - 1)), sem((S, Q, Z - 1)),
        sem((S, Q, 2)), sem((S, Q, 2)),
        sem((S, Q, Z - 1)), sem((S, Q, Z - 1)),
        sem((S, T - 1)), sem((S, T - 1)),
        sem((S,)), sem((S,)),
        sem((S, DP - 1)), sem((S, DP - 1)),
        sem((S, DP - 1)), sem((S, DP - 1)),
        sem((DP - 1,)), sem((DP - 1,)),
    ]
    gi, gow, pg = pl.pallas_call(
        kernel,
        out_shape=(
            jax.ShapeDtypeStruct((S, R, D), BF16),
            jax.ShapeDtypeStruct((X, X), BF16),
            jax.ShapeDtypeStruct((8, C), F32),
        ),
        in_specs=[any_spec, any_spec, any_spec, any_spec] + [vmem_spec] * 6,
        out_specs=(any_spec, any_spec, any_spec),
        scratch_shapes=scratch,
        compiler_params=pltpu.CompilerParams(
            collective_id=0, has_side_effects=True, vmem_limit_bytes=64 * 2**20 - 2**16
        ),
        name="mixer_backward",
    )(cot, saved_u[0], in_weight[0], out_weight[0], jnp.swapaxes(dt_raw[0], 1, 2), conv_weight[0], conv_bias, a_log, dt_bias, d_skip)
    outs = pl.pallas_call(
        finish,
        out_shape=(
            jax.ShapeDtypeStruct((S, R, D), BF16),
            jax.ShapeDtypeStruct((X, X), BF16),
            jax.ShapeDtypeStruct((4, C), F32),
            jax.ShapeDtypeStruct((1, C), F32),
            jax.ShapeDtypeStruct((1, HEADS), F32),
            jax.ShapeDtypeStruct((1, HEADS), F32),
            jax.ShapeDtypeStruct((1, HEADS), F32),
        ),
        in_specs=[any_spec] * 3,
        out_specs=(vmem_spec,) * 7,
        scratch_shapes=[pltpu.VMEM((8, C), F32), sem((3,))],
        compiler_params=pltpu.CompilerParams(vmem_limit_bytes=64 * 2**20 - 2**16),
        name="finish",
    )(gi, gow, pg)
    gi, gow, cw, cb, al, db, sk = outs
    return gi[None], gow[None], cw[None], cb, al, db, sk


def solution(mesh):
    return jax.shard_map(
        shards,
        mesh=mesh,
        in_specs=(
            P("dp", "tensor", None),
            P("pipe", "dp", None, "tensor"),
            P("pipe", "dp", None, "tensor"),
            P("pipe", None, "tensor"),
            P("pipe", "tensor", None),
            P("pipe", None, "tensor"),
            P("pipe", "tensor"),
            P("pipe", "tensor"),
            P("pipe", "tensor"),
            P("pipe", "tensor"),
        ),
        out_specs=(
            P("pipe", "dp", "tensor", None),
            P("pipe", "tensor", "dp"),
            P("pipe", None, "tensor"),
            P("pipe", "tensor"),
            P("pipe", "tensor"),
            P("pipe", "tensor"),
            P("pipe", "tensor"),
        ),
        check_vma=False,
    )
```

```python
import jax
import jax.numpy as jnp
from jax import lax
from jax.experimental import pallas as pl
from jax.experimental.pallas import tpu as pltpu
from jax.sharding import PartitionSpec as P

F32 = jnp.float32
BF16 = jnp.bfloat16
MESH = pl.DeviceIdType.MESH
NT = (((1,), (1,)), ((), ()))
NN = (((1,), (0,)), ((), ()))
TN = (((0,), (0,)), ((), ()))
HIGH = lax.Precision.HIGHEST

L = 192
D = 4096
X = 1024
C = 1536
HEADS = 16
PAIRS = 8
N = 256
T = 8
Z = 4
Q = 4
B = Z * Q
W = D // B
R = L // T
DP = 4
S = 2
TOP = 8


def dot(a, b, dims, precision=None):
    return lax.dot_general(a, b, dims, preferred_element_type=F32, precision=precision)


def iota(shape, axis):
    return lax.broadcasted_iota(jnp.int32, shape, axis)


def lanes(j, width=128):
    return pl.ds(pl.multiple_of(j * width, width), width)


def loop(count, body):
    def step(i, carry):
        body(i)
        return carry

    lax.fori_loop(0, count, step, 0)


def kernel(
    cot_ref, u_hbm, win_hbm, wout_hbm, dtr_ref, cw_ref, cb_ref, al_ref, db_ref, sk_ref,
    gi_out, gow_out, pg_out,
    win, wout, u_ref, upad, sp, abf, xst, mt, est, y0, yb, sT, scol, dtc, sgc, skl,
    cbuf, crecv, gbuf, gcols, dyacc, dybf, dx0, dcb, dcpad, own,
    sbuf, rbuf, psum, pbuf, orow, obuf, gi_v, pg, pgr, pgsum,
    loc, cs_s, cs_r, a_s, a_r, b_s, b_r, c_s, c_r, f_s, f_r, o_s, o_r,
    yb_s, yb_r, gx_s, gx_r, pg_s, pg_r,
):
    p = lax.axis_index("pipe")
    t = lax.axis_index("tensor")
    d = lax.axis_index("dp")
    first = p == 3
    last = p == 0

    def peer(i):
        return (p, lax.rem(t + i, T), d)

    z = t // 2
    side = t % 2
    other = 1 - side

    def above(i):
        return lax.rem(z + i, Z)

    def column(i):
        return (p, 2 * above(i) + side, d)

    def replica(i):
        return (p, t, lax.rem(d + i, DP))

    def local(src, dst, i):
        return pltpu.make_async_copy(src, dst, loc.at[i])

    def remote(src, dst, ssem, rsem, to):
        return pltpu.make_async_remote_copy(
            src_ref=src, dst_ref=dst, send_sem=ssem, recv_sem=rsem, device_id=to, device_id_type=MESH
        )

    local(u_hbm, u_ref, 0).start()
    local(cot_ref, cbuf, 6).start()
    local(wout_hbm, wout, 1).start()
    local(win_hbm, win, 2).start()

    barrier = pltpu.get_barrier_semaphore()
    for i in range(1, T):
        pl.semaphore_signal(barrier, inc=1, device_id=peer(i), device_id_type=MESH)
    for i in range(1, DP):
        pl.semaphore_signal(barrier, inc=1, device_id=replica(i), device_id_type=MESH)

    @pl.when(p > 0)
    def _():
        for i in range(2):
            pl.semaphore_signal(barrier, inc=1, device_id=(p - 1, 2 * z + i, d), device_id_type=MESH)

    @pl.when(p < 3)
    def _():
        for i in range(2):
            pl.semaphore_signal(barrier, inc=1, device_id=(p + 1, 2 * z + i, d), device_id_type=MESH)

    middle = jnp.logical_and(p > 0, p < 3)

    @pl.when(middle)
    def _():
        pl.semaphore_wait(barrier, T - 1 + DP - 1 + 4)

    @pl.when(jnp.logical_not(middle))
    def _():
        pl.semaphore_wait(barrier, T - 1 + DP - 1 + 2)

    def cot_copy(s, i):
        return remote(cbuf.at[s], crecv.at[s, t], cs_s.at[s, i - 1], cs_r.at[s, i - 1], peer(i))

    def cot_arrival(s, i):
        src = lax.rem(t + T - i, T)
        return remote(cbuf.at[s], crecv.at[s, src], cs_s.at[s, i - 1], cs_r.at[s, i - 1], peer(i))

    def cot_send(s):
        @pl.when(first)
        def _():
            for i in range(1, T):
                cot_copy(s, i).start()
            crecv[s, t] = cbuf[s]

    local(cot_ref, cbuf, 6).wait()
    cot_send(0)

    rr = iota((L, L), 0)
    tt = iota((L, L), 1)
    upper = (rr <= tt).astype(F32)
    eye = (iota((HEADS, HEADS), 0) == iota((HEADS, HEADS), 1)).astype(F32)

    def upright(row):
        return jnp.sum(eye * row, axis=1, keepdims=True)

    rate = -jnp.exp(al_ref[...])
    spread = (iota((HEADS, X), 0) == iota((HEADS, X), 1) // 64).astype(F32)
    skl[...] = dot(sk_ref[...], spread, NN, HIGH)

    def forward(s):
        upad[s, 0:TOP, :] = jnp.zeros((TOP, C), F32)

        def conv(j):
            at = lanes(j)
            upad[s, TOP : TOP + L, at] = u_ref[s, :, at].astype(F32)
            c = jnp.broadcast_to(cb_ref[:, at], (L, 128))
            for k in range(4):
                c = c + cw_ref[k : k + 1, at] * upad[s, TOP - 3 + k : TOP - 3 + k + L, at]
            sig = 1.0 / (1.0 + jnp.exp(-c))
            sp[s, :, at] = sig * (1.0 + c * (1.0 - sig))
            abf[s, :, at] = (c * sig).astype(BF16)

        loop(C // 128, conv)
        raw = dtr_ref[s] + upright(db_ref[...])
        dt = jnp.maximum(raw, 0.0) + jnp.log1p(jnp.exp(-jnp.abs(raw)))
        total = dot(dt * upright(rate), upper, NN, HIGH)
        sT[...] = total
        scol[...] = dot(total, eye, TN, HIGH)
        dtc[s] = dot(dt, eye, TN, HIGH)
        sgc[s] = dot(1.0 / (1.0 + jnp.exp(-raw)), eye, TN, HIGH)
        dcb[...] = dot(abf[s, :, X : X + N], abf[s, :, X + N : X + 2 * N], NT)

        def pair(j):
            at = lanes(j)
            x2 = abf[s, :, at].astype(F32)
            even = iota((L, 128), 1) < 64
            xst[s, j, 0:L, :] = jnp.where(even, x2, 0.0).astype(BF16)
            xst[s, j, L : 2 * L, :] = jnp.where(even, 0.0, x2).astype(BF16)
            causal = iota((L, L), 1) >= iota((L, L), 0)
            head = iota((L, HEADS), 1)
            for e in range(2):
                h = 2 * j + e
                s_r = jnp.sum(jnp.where(head == h, scol[...], 0.0), axis=1, keepdims=True)
                dt_r = jnp.sum(jnp.where(head == h, dtc[s], 0.0), axis=1, keepdims=True)
                decay = jnp.exp(jnp.minimum(sT[pl.ds(h, 1), :] - s_r, 0.0)) * dt_r
                decay = jnp.where(causal, decay, 0.0)
                est[s, j, e * L : (e + 1) * L, :] = decay.astype(BF16)
                mt[s, j, e * L : (e + 1) * L, :] = (decay * dcb[...]).astype(BF16)
            y2 = dot(mt[s, j], xst[s, j], TN)
            y0[s, :, at] = y2
            yb[d, s, :, at] = (y2 + skl[:, at] * x2).astype(BF16)

        loop(PAIRS, pair)

    def yb_copy(s, i):
        return remote(yb.at[d, s], yb.at[d, s], yb_s.at[s, i - 1], yb_r.at[s, i - 1], replica(i))

    def yb_arrival(s, i):
        src = lax.rem(d + DP - i, DP)
        return remote(yb.at[src, s], yb.at[src, s], yb_s.at[s, i - 1], yb_r.at[s, i - 1], replica(i))

    local(u_hbm, u_ref, 0).wait()
    forward(0)
    cot_send(1)
    forward(1)
    for s in range(S):
        for i in range(1, DP):
            yb_copy(s, i).start()

    local(wout_hbm, wout, 1).wait()

    def b_copy(s, q, to):
        return remote(
            psum.at[s, q], pbuf.at[s, q, side], b_s.at[s, q, to], b_r.at[s, q, side],
            (p - 1, 2 * z + to, d),
        )

    def b_arrival(s, q, src):
        return remote(
            psum.at[s, q], pbuf.at[s, q, src], b_s.at[s, q, src], b_r.at[s, q, src],
            (p + 1, 2 * z + src, d),
        )

    def c_copy(s, q, i):
        at = gbuf.at[s, Q * z + q]
        return remote(at, at, c_s.at[s, q, i - 1], c_r.at[s, q, i - 1], column(i))

    def c_arrival(s, q, i):
        at = gbuf.at[s, Q * above(Z - i) + q]
        return remote(at, at, c_s.at[s, q, i - 1], c_r.at[s, q, i - 1], column(i))

    def gather(s, q):
        @pl.when(p < 3)
        def _():
            for src in range(2):
                b_arrival(s, q, src).wait_recv()

            def block(j):
                at = lanes(j)
                total = pbuf[s, q, 0, :, at].astype(F32) + pbuf[s, q, 1, :, at].astype(F32)
                gbuf[s, Q * z + q, :, at] = total.astype(BF16)

            loop(W // 128, block)
            for i in (2, 1, 3):
                c_copy(s, q, i).start()

    def gx_copy(s, i):
        to = lax.rem(d + i, DP)
        return remote(
            gbuf.at[s, pl.ds(Q * to, Q)], gcols.at[d, s], gx_s.at[s, i - 1], gx_r.at[s, i - 1], replica(i)
        )

    def gx_arrival(s, i):
        src = lax.rem(d + DP - i, DP)
        return remote(
            gbuf.at[s, pl.ds(0, Q)], gcols.at[src, s], gx_s.at[s, i - 1], gx_r.at[s, i - 1], replica(i)
        )

    def grad_mix(s):
        @pl.when(first)
        def _():
            for i in range(1, T):
                cot_arrival(s, i).wait_recv()

            def block(k):
                rows = crecv[s, :, :, lanes(k, W)].astype(F32)
                gbuf[s, k] = rows.reshape(L, W).astype(BF16)

            loop(B, block)

        for q in range(Q):

            @pl.when(p < 3)
            def _():
                for i in range(1, Z):
                    c_arrival(s, q, i).wait_recv()

            part = None
            for i in range(Z):
                k = Q * above(Z - i) + q
                term = dot(gbuf[s, k], wout[:, lanes(k, W)], NT)
                part = term if part is None else part + term
            if q == 0:
                dyacc[...] = part
            elif q < Q - 1:
                dyacc[...] += part
            else:
                dybf[s] = (dyacc[...] + part).astype(BF16)
        for i in range(1, DP):
            gx_copy(s, i).start()
        gcols[d, s] = gbuf[s, pl.ds(Q * d, Q)]

    def o_copy(s):
        return remote(orow.at[s], gi_v.at[s], o_s.at[s], o_r.at[s], (p + 1, t, d))

    def share(s):
        @pl.when(p < 3)
        def _():
            for k in range(B):
                rows = gbuf[s, k].astype(F32).reshape(T, R, W)
                mine = jnp.where(t == 0, rows[0], 0.0)
                for i in range(1, T):
                    mine = jnp.where(t == i, rows[i], mine)
                orow[s, :, k * W : (k + 1) * W] = mine.astype(BF16)
            o_copy(s).start()

    def pull(s):
        dcb[...] = jnp.zeros_like(dcb)

        def pair(j):
            at = lanes(j)
            dy2 = dybf[s, :, at]
            dm = dot(xst[s, j], dy2, NT)
            dcb[...] += dm[:L] * est[s, j, 0:L, :].astype(F32) + dm[L:] * est[s, j, L : 2 * L, :].astype(F32)
            dx = dot(mt[s, j], dy2, NN)
            dx = jnp.where(iota((L, 128), 1) < 64, dx[:L], dx[L:])
            dx0[s, :, at] = dx
            dcpad[s, 0:L, at] = (dx + skl[:, at] * dy2.astype(F32)) * sp[s, :, at]

        loop(PAIRS, pair)
        low = dcb[...].astype(BF16)
        dcpad[s, 0:L, X : X + N] = dot(low, abf[s, :, X + N : X + 2 * N], NN) * sp[s, :, X : X + N]
        dcpad[s, 0:L, X + N : X + 2 * N] = (
            dot(low, abf[s, :, X : X + N], TN) * sp[s, :, X + N : X + 2 * N]
        )

        def conv(j):
            at = lanes(j)
            du = cw_ref[3:4, at] * dcpad[s, 0:L, at]
            for k in range(3):
                du = du + cw_ref[k : k + 1, at] * dcpad[s, 3 - k : 3 - k + L, at]
            u_ref[0, :, at] = du.astype(BF16)

        loop(C // 128, conv)

    def a_copy(s, q, i):
        return remote(sbuf.at[q, i - 1], rbuf.at[s, q, i - 1], a_s.at[s, q, i - 1], a_r.at[s, q, i - 1], column(i))

    def scatter(s):
        for q in range(Q):
            for i in (2, 1, 3, 0):
                part = dot(u_ref[0], win[lanes(Q * above(i) + q, W), :], NT)
                if i:
                    sbuf[q, i - 1] = part.astype(BF16)
                    a_copy(s, q, i).start()
                else:
                    own[q] = part

    def f_copy(s, i):
        return remote(obuf.at[s, lax.rem(t + i, T)], crecv.at[s, t, :, pl.ds(0, Q * W)], f_s.at[s, i - 1], f_r.at[s, i - 1], peer(i))

    def f_arrival(s, i):
        at = crecv.at[s, lax.rem(t + T - i, T), :, pl.ds(0, Q * W)]
        return remote(obuf.at[s, t], at, f_s.at[s, i - 1], f_r.at[s, i - 1], peer(i))

    def combine(s, q):
        for i in range(1, Z):
            a_copy(s, q, i).wait_recv()

        for j in range(W // 128):
            at = slice(j * 128, (j + 1) * 128)
            mine = side == q // (Q // 2)
            total = own[q, :, at] + jnp.where(mine, gbuf[s, Q * z + q, :, at].astype(F32), 0.0)
            for i in range(Z - 1):
                total = total + rbuf[s, q, i, :, at].astype(F32)
            psum[s, q, :, at] = total.astype(BF16)

            @pl.when(last)
            def _():
                obuf[s, :, :, q * W + j * 128 : q * W + (j + 1) * 128] = total.reshape(T, R, 128).astype(BF16)

        @pl.when(p > 0)
        def _():
            b_copy(s, q, other).start()
            b_copy(s, q, side).start()

        for i in range(1, Z):
            a_copy(s, q, i).wait_send()

    def rows_out(s):
        for i in range(1, T):
            f_copy(s, i).start()
        crecv[s, t, :, 0 : Q * W] = obuf[s, t]

    def parameters(s):
        def two(value):
            high = value.astype(BF16)
            rest = (value - high.astype(F32)).astype(BF16)
            return jnp.concatenate([high, rest], axis=1)

        def pair(j, carry):
            d_s, d_t, d_k = carry
            at = lanes(j)
            dy2 = dybf[s, :, at].astype(F32)
            x2 = abf[s, :, at].astype(F32)
            inner = x2 * dx0[s, :, at]
            outer = dy2 * y0[s, :, at] - inner
            lane = iota((2 * 128, HEADS), 0)
            lane = jnp.where(lane >= 128, lane - 128, lane)
            head = 2 * j + jnp.where(lane >= 64, 1, 0)
            pick = (head == iota((2 * 128, HEADS), 1)).astype(BF16)
            skip = jnp.broadcast_to(jnp.sum(dy2 * x2, axis=0, keepdims=True), (8, 128))
            return (
                d_s + dot(two(outer), pick, NN),
                d_t + dot(two(inner), pick, NN),
                d_k + dot(two(skip), pick, NN),
            )

        zero = jnp.zeros((L, HEADS), F32)
        d_s, d_t, d_k = lax.fori_loop(0, PAIRS, pair, (zero, zero, jnp.zeros((8, HEADS), F32)))
        later = dot((iota((L, L), 0) <= iota((L, L), 1)).astype(F32), d_s, NN, HIGH)
        dt = dtc[s]
        g_al = jnp.sum(later * dt, axis=0, keepdims=True) * rate
        g_db = jnp.sum((d_t / dt + later * rate) * sgc[s], axis=0, keepdims=True)
        small = (g_al, g_db, d_k[0:1])

        def conv(j):
            at = lanes(j)
            dc = dcpad[s, 0:L, at]
            rows = []
            for k in range(4):
                rows.append(jnp.sum(dc * upad[s, TOP - 3 + k : TOP - 3 + k + L, at], axis=0, keepdims=True))
            rows.append(jnp.sum(dc, axis=0, keepdims=True))
            rows.append(jnp.zeros((3, 128), F32))
            value = jnp.concatenate(rows, axis=0)
            pg[:, at] = value if s == 0 else pg[:, at] + value

        loop(C // 128, conv)
        for i in range(3):
            if s == 0:
                pg[5 + i : 6 + i, 0:HEADS] = small[i]
            else:
                pg[5 + i : 6 + i, 0:HEADS] += small[i]

    def pg_copy(i):
        return remote(pg, pgr.at[d], pg_s.at[i - 1], pg_r.at[i - 1], replica(i))

    def pg_arrival(i):
        src = lax.rem(d + DP - i, DP)
        return remote(pg, pgr.at[src], pg_s.at[i - 1], pg_r.at[i - 1], replica(i))

    def projection():
        for s in range(S):
            for i in range(1, DP):
                yb_arrival(s, i).wait_recv()
                gx_arrival(s, i).wait_recv()

        for k in range(2):

            def block(j):
                rows = yb[:, :, :, lanes(j, 256)].reshape(DP * S * L, 256)
                cols = jnp.concatenate(
                    [gcols[:, :, 2 * k + e].reshape(DP * S * L, W) for e in range(2)], axis=1
                )
                win[lanes(j, 256), 2 * k * W : 2 * (k + 1) * W] = dot(rows, cols, TN).astype(BF16)

            loop(X // 256, block)
        local(win.at[pl.ds(0, X), pl.ds(0, X)], gow_out, 3).start()

    dcpad[:, L : L + TOP, :] = jnp.zeros((S, TOP, C), F32)
    for q in range(Q):
        gather(0, q)
    grad_mix(0)
    pull(0)
    local(win_hbm, win, 2).wait()
    scatter(0)
    for q in range(Q):
        gather(1, q)
    for q in range(Q):
        combine(0, q)

    @pl.when(last)
    def _():
        rows_out(0)


    @pl.when(p < 3)
    def _():
        share(0)
        parameters(0)

    grad_mix(1)
    pull(1)
    scatter(1)

    @pl.when(first)
    def _():
        parameters(0)

    def sum_parameters():
        share(1)
        parameters(1)
        pgr[d] = pg[...]
        for i in range(1, DP):
            pg_copy(i).start()

    @pl.when(last)
    def _():
        sum_parameters()

    for q in range(Q):
        combine(1, q)

    @pl.when(last)
    def _():
        rows_out(1)

    @pl.when(p > 0)
    def _():
        sum_parameters()

    projection()

    for i in range(1, DP):
        pg_arrival(i).wait_recv()
    total = pgr[0]
    for i in range(1, DP):
        total = total + pgr[i]
    pgsum[...] = total
    local(pgsum, pg_out, 4).start()

    @pl.when(last)
    def _():
        for s in range(S):
            for i in range(1, T):
                f_arrival(s, i).wait_recv()
            for k in range(Z):
                a, b = crecv[s, 2 * k, :, 0 : Q * W], crecv[s, 2 * k + 1, :, 0 : Q * W]
                gi_v[s, :, k * Q * W : (k + 1) * Q * W] = (a.astype(F32) + b.astype(F32)).astype(BF16)

    @pl.when(p > 0)
    def _():
        for s in range(S):
            remote(orow.at[s], gi_v.at[s], o_s.at[s], o_r.at[s], (p - 1, t, d)).wait_recv()

    local(gi_v, gi_out, 5).start()

    @pl.when(first)
    def _():
        for s in range(S):
            for i in range(1, T):
                cot_copy(s, i).wait_send()

    @pl.when(p < 3)
    def _():
        for s in range(S):
            o_copy(s).wait_send()
            for q in range(Q):
                for i in range(1, Z):
                    c_copy(s, q, i).wait_send()

    @pl.when(p > 0)
    def _():
        for s in range(S):
            for q in range(Q):
                for to in range(2):
                    b_copy(s, q, to).wait_send()

    @pl.when(last)
    def _():
        for s in range(S):
            for i in range(1, T):
                f_copy(s, i).wait_send()

    for s in range(S):
        for i in range(1, DP):
            yb_copy(s, i).wait_send()
            gx_copy(s, i).wait_send()
    for i in range(1, DP):
        pg_copy(i).wait_send()
    local(win.at[pl.ds(0, X), pl.ds(0, X)], gow_out, 3).wait()
    local(pgsum, pg_out, 4).wait()
    local(gi_v, gi_out, 5).wait()


def finish(gi_ref, gow_ref, pg_ref, gi, gow, cw, cb, al, db, sk, pg, sems):
    copies = [
        pltpu.make_async_copy(src, dst, sems.at[i])
        for i, (src, dst) in enumerate(((gow_ref, gow), (gi_ref, gi), (pg_ref, pg)))
    ]
    for copy in copies:
        copy.start()
    copies[2].wait()
    cw[...] = pg[0:4, :]
    cb[...] = pg[4:5, :]
    al[...] = pg[5:6, 0:HEADS]
    db[...] = pg[6:7, 0:HEADS]
    sk[...] = pg[7:8, 0:HEADS]
    copies[1].wait()
    copies[0].wait()


def shards(cot, saved_u, dt_raw, in_weight, out_weight, conv_weight, conv_bias, a_log, dt_bias, d_skip):
    any_spec = pl.BlockSpec(memory_space=pl.ANY)
    vmem_spec = pl.BlockSpec(memory_space=pltpu.VMEM)
    sem = pltpu.SemaphoreType.DMA
    scratch = [
        pltpu.VMEM((D, C), BF16),
        pltpu.VMEM((X, D), BF16),
        pltpu.VMEM((S, L, C), BF16),
        pltpu.VMEM((S, L + 2 * TOP, C), F32),
        pltpu.VMEM((S, L, C), F32),
        pltpu.VMEM((S, L, C), BF16),
        pltpu.VMEM((S, PAIRS, 2 * L, 128), BF16),
        pltpu.VMEM((S, PAIRS, 2 * L, L), BF16),
        pltpu.VMEM((S, PAIRS, 2 * L, L), BF16),
        pltpu.VMEM((S, L, X), F32),
        pltpu.VMEM((DP, S, L, X), BF16),
        pltpu.VMEM((HEADS, L), F32),
        pltpu.VMEM((L, HEADS), F32),
        pltpu.VMEM((S, L, HEADS), F32),
        pltpu.VMEM((S, L, HEADS), F32),
        pltpu.VMEM((1, X), F32),
        pltpu.VMEM((S, R, D), BF16),
        pltpu.VMEM((S, T, R, D), BF16),
        pltpu.VMEM((S, B, L, W), BF16),
        pltpu.VMEM((DP, S, Q, L, W), BF16),
        pltpu.VMEM((L, X), F32),
        pltpu.VMEM((S, L, X), BF16),
        pltpu.VMEM((S, L, X), F32),
        pltpu.VMEM((L, L), F32),
        pltpu.VMEM((S, L + TOP, C), F32),
        pltpu.VMEM((Q, L, W), F32),
        pltpu.VMEM((Q, Z - 1, L, W), BF16),
        pltpu.VMEM((S, Q, Z - 1, L, W), BF16),
        pltpu.VMEM((S, Q, L, W), BF16),
        pltpu.VMEM((S, Q, 2, L, W), BF16),
        pltpu.VMEM((S, R, D), BF16),
        pltpu.VMEM((S, T, R, Q * W), BF16),
        pltpu.VMEM((S, R, D), BF16),
        pltpu.VMEM((8, C), F32),
        pltpu.VMEM((DP, 8, C), F32),
        pltpu.VMEM((8, C), F32),
        sem((7,)),
        sem((S, T - 1)), sem((S, T - 1)),
        sem((S, Q, Z - 1)), sem((S, Q, Z - 1)),
        sem((S, Q, 2)), sem((S, Q, 2)),
        sem((S, Q, Z - 1)), sem((S, Q, Z - 1)),
        sem((S, T - 1)), sem((S, T - 1)),
        sem((S,)), sem((S,)),
        sem((S, DP - 1)), sem((S, DP - 1)),
        sem((S, DP - 1)), sem((S, DP - 1)),
        sem((DP - 1,)), sem((DP - 1,)),
    ]
    gi, gow, pg = pl.pallas_call(
        kernel,
        out_shape=(
            jax.ShapeDtypeStruct((S, R, D), BF16),
            jax.ShapeDtypeStruct((X, X), BF16),
            jax.ShapeDtypeStruct((8, C), F32),
        ),
        in_specs=[any_spec, any_spec, any_spec, any_spec] + [vmem_spec] * 6,
        out_specs=(any_spec, any_spec, any_spec),
        scratch_shapes=scratch,
        compiler_params=pltpu.CompilerParams(
            collective_id=0, has_side_effects=True, vmem_limit_bytes=64 * 2**20 - 2**16
        ),
        name="mixer_backward",
    )(cot, saved_u[0], in_weight[0], out_weight[0], jnp.swapaxes(dt_raw[0], 1, 2), conv_weight[0], conv_bias, a_log, dt_bias, d_skip)
    outs = pl.pallas_call(
        finish,
        out_shape=(
            jax.ShapeDtypeStruct((S, R, D), BF16),
            jax.ShapeDtypeStruct((X, X), BF16),
            jax.ShapeDtypeStruct((4, C), F32),
            jax.ShapeDtypeStruct((1, C), F32),
            jax.ShapeDtypeStruct((1, HEADS), F32),
            jax.ShapeDtypeStruct((1, HEADS), F32),
            jax.ShapeDtypeStruct((1, HEADS), F32),
        ),
        in_specs=[any_spec] * 3,
        out_specs=(vmem_spec,) * 7,
        scratch_shapes=[pltpu.VMEM((8, C), F32), sem((3,))],
        compiler_params=pltpu.CompilerParams(vmem_limit_bytes=64 * 2**20 - 2**16),
        name="finish",
    )(gi, gow, pg)
    gi, gow, cw, cb, al, db, sk = outs
    return gi[None], gow[None], cw[None], cb, al, db, sk


def solution(mesh):
    return jax.shard_map(
        shards,
        mesh=mesh,
        in_specs=(
            P("dp", "tensor", None),
            P("pipe", "dp", None, "tensor"),
            P("pipe", "dp", None, "tensor"),
            P("pipe", None, "tensor"),
            P("pipe", "tensor", None),
            P("pipe", None, "tensor"),
            P("pipe", "tensor"),
            P("pipe", "tensor"),
            P("pipe", "tensor"),
            P("pipe", "tensor"),
        ),
        out_specs=(
            P("pipe", "dp", "tensor", None),
            P("pipe", "tensor", "dp"),
            P("pipe", None, "tensor"),
            P("pipe", "tensor"),
            P("pipe", "tensor"),
            P("pipe", "tensor"),
            P("pipe", "tensor"),
        ),
        check_vma=False,
    )
```

```python
import jax
import jax.numpy as jnp
from jax import lax
from jax.experimental import pallas as pl
from jax.experimental.pallas import tpu as pltpu
from jax.sharding import PartitionSpec as P

F32 = jnp.float32
BF16 = jnp.bfloat16
MESH = pl.DeviceIdType.MESH
NT = (((1,), (1,)), ((), ()))
NN = (((1,), (0,)), ((), ()))
TN = (((0,), (0,)), ((), ()))
HIGH = lax.Precision.HIGHEST

L = 192
D = 4096
X = 1024
C = 1536
HEADS = 16
PAIRS = 8
N = 256
T = 8
Z = 4
Q = 4
B = Z * Q
W = D // B
R = L // T
DP = 4
S = 2
TOP = 8


def dot(a, b, dims, precision=None):
    return lax.dot_general(a, b, dims, preferred_element_type=F32, precision=precision)


def iota(shape, axis):
    return lax.broadcasted_iota(jnp.int32, shape, axis)


def lanes(j, width=128):
    return pl.ds(pl.multiple_of(j * width, width), width)


def loop(count, body):
    def step(i, carry):
        body(i)
        return carry

    lax.fori_loop(0, count, step, 0)


def kernel(
    cot_ref, u_hbm, win_hbm, wout_hbm, dtr_ref, cw_ref, cb_ref, al_ref, db_ref, sk_ref,
    gi_out, gow_out, pg_out,
    win, wout, u_ref, upad, sp, abf, xst, mt, est, y0, yb, sT, scol, dtc, sgc, skl,
    cbuf, crecv, gbuf, gcols, dyacc, dybf, dx0, dcb, dcpad, own,
    sbuf, rbuf, psum, pbuf, orow, obuf, gi_v, pg, pgr, pgsum,
    loc, cs_s, cs_r, a_s, a_r, b_s, b_r, c_s, c_r, f_s, f_r, o_s, o_r,
    yb_s, yb_r, gx_s, gx_r, pg_s, pg_r,
):
    p = lax.axis_index("pipe")
    t = lax.axis_index("tensor")
    d = lax.axis_index("dp")
    first = p == 3
    last = p == 0

    def peer(i):
        return (p, lax.rem(t + i, T), d)

    z = t // 2
    side = t % 2
    other = 1 - side

    def above(i):
        return lax.rem(z + i, Z)

    def column(i):
        return (p, 2 * above(i) + side, d)

    def replica(i):
        return (p, t, lax.rem(d + i, DP))

    def local(src, dst, i):
        return pltpu.make_async_copy(src, dst, loc.at[i])

    def remote(src, dst, ssem, rsem, to):
        return pltpu.make_async_remote_copy(
            src_ref=src, dst_ref=dst, send_sem=ssem, recv_sem=rsem, device_id=to, device_id_type=MESH
        )

    local(u_hbm, u_ref, 0).start()
    local(cot_ref, cbuf, 6).start()
    local(wout_hbm, wout, 1).start()
    local(win_hbm, win, 2).start()

    barrier = pltpu.get_barrier_semaphore()
    for i in range(1, T):
        pl.semaphore_signal(barrier, inc=1, device_id=peer(i), device_id_type=MESH)
    for i in range(1, DP):
        pl.semaphore_signal(barrier, inc=1, device_id=replica(i), device_id_type=MESH)

    @pl.when(p > 0)
    def _():
        for i in range(2):
            pl.semaphore_signal(barrier, inc=1, device_id=(p - 1, 2 * z + i, d), device_id_type=MESH)

    @pl.when(p < 3)
    def _():
        for i in range(2):
            pl.semaphore_signal(barrier, inc=1, device_id=(p + 1, 2 * z + i, d), device_id_type=MESH)

    middle = jnp.logical_and(p > 0, p < 3)

    @pl.when(middle)
    def _():
        pl.semaphore_wait(barrier, T - 1 + DP - 1 + 4)

    @pl.when(jnp.logical_not(middle))
    def _():
        pl.semaphore_wait(barrier, T - 1 + DP - 1 + 2)

    def cot_copy(s, i):
        return remote(cbuf.at[s], crecv.at[s, t], cs_s.at[s, i - 1], cs_r.at[s, i - 1], peer(i))

    def cot_arrival(s, i):
        src = lax.rem(t + T - i, T)
        return remote(cbuf.at[s], crecv.at[s, src], cs_s.at[s, i - 1], cs_r.at[s, i - 1], peer(i))

    def cot_send(s):
        @pl.when(first)
        def _():
            for i in range(1, T):
                cot_copy(s, i).start()
            crecv[s, t] = cbuf[s]

    local(cot_ref, cbuf, 6).wait()
    cot_send(0)

    rr = iota((L, L), 0)
    tt = iota((L, L), 1)
    upper = (rr <= tt).astype(F32)
    eye = (iota((HEADS, HEADS), 0) == iota((HEADS, HEADS), 1)).astype(F32)

    def upright(row):
        return jnp.sum(eye * row, axis=1, keepdims=True)

    rate = -jnp.exp(al_ref[...])
    spread = (iota((HEADS, X), 0) == iota((HEADS, X), 1) // 64).astype(F32)
    skl[...] = dot(sk_ref[...], spread, NN, HIGH)

    def forward(s):
        upad[s, 0:TOP, :] = jnp.zeros((TOP, C), F32)

        def conv(j):
            at = lanes(j)
            upad[s, TOP : TOP + L, at] = u_ref[s, :, at].astype(F32)
            c = jnp.broadcast_to(cb_ref[:, at], (L, 128))
            for k in range(4):
                c = c + cw_ref[k : k + 1, at] * upad[s, TOP - 3 + k : TOP - 3 + k + L, at]
            sig = 1.0 / (1.0 + jnp.exp(-c))
            sp[s, :, at] = sig * (1.0 + c * (1.0 - sig))
            abf[s, :, at] = (c * sig).astype(BF16)

        loop(C // 128, conv)
        raw = dtr_ref[s] + upright(db_ref[...])
        dt = jnp.maximum(raw, 0.0) + jnp.log1p(jnp.exp(-jnp.abs(raw)))
        total = dot(dt * upright(rate), upper, NN, HIGH)
        sT[...] = total
        scol[...] = dot(total, eye, TN, HIGH)
        dtc[s] = dot(dt, eye, TN, HIGH)
        sgc[s] = dot(1.0 / (1.0 + jnp.exp(-raw)), eye, TN, HIGH)
        dcb[...] = dot(abf[s, :, X : X + N], abf[s, :, X + N : X + 2 * N], NT)

        def pair(j):
            at = lanes(j)
            x2 = abf[s, :, at].astype(F32)
            even = iota((L, 128), 1) < 64
            xst[s, j, 0:L, :] = jnp.where(even, x2, 0.0).astype(BF16)
            xst[s, j, L : 2 * L, :] = jnp.where(even, 0.0, x2).astype(BF16)
            causal = iota((L, L), 1) >= iota((L, L), 0)
            head = iota((L, HEADS), 1)
            for e in range(2):
                h = 2 * j + e
                s_r = jnp.sum(jnp.where(head == h, scol[...], 0.0), axis=1, keepdims=True)
                dt_r = jnp.sum(jnp.where(head == h, dtc[s], 0.0), axis=1, keepdims=True)
                decay = jnp.exp(jnp.minimum(sT[pl.ds(h, 1), :] - s_r, 0.0)) * dt_r
                decay = jnp.where(causal, decay, 0.0)
                est[s, j, e * L : (e + 1) * L, :] = decay.astype(BF16)
                mt[s, j, e * L : (e + 1) * L, :] = (decay * dcb[...]).astype(BF16)
            y2 = dot(mt[s, j], xst[s, j], TN)
            y0[s, :, at] = y2
            yb[d, s, :, at] = (y2 + skl[:, at] * x2).astype(BF16)

        loop(PAIRS, pair)

    def yb_copy(s, i):
        return remote(yb.at[d, s], yb.at[d, s], yb_s.at[s, i - 1], yb_r.at[s, i - 1], replica(i))

    def yb_arrival(s, i):
        src = lax.rem(d + DP - i, DP)
        return remote(yb.at[src, s], yb.at[src, s], yb_s.at[s, i - 1], yb_r.at[s, i - 1], replica(i))

    local(u_hbm, u_ref, 0).wait()
    forward(0)
    cot_send(1)
    forward(1)
    for s in range(S):
        for i in range(1, DP):
            yb_copy(s, i).start()

    local(wout_hbm, wout, 1).wait()

    def b_copy(s, q, to):
        return remote(
            psum.at[s, q], pbuf.at[s, q, side], b_s.at[s, q, to], b_r.at[s, q, side],
            (p - 1, 2 * z + to, d),
        )

    def b_arrival(s, q, src):
        return remote(
            psum.at[s, q], pbuf.at[s, q, src], b_s.at[s, q, src], b_r.at[s, q, src],
            (p + 1, 2 * z + src, d),
        )

    def c_copy(s, q, i):
        at = gbuf.at[s, Q * z + q]
        return remote(at, at, c_s.at[s, q, i - 1], c_r.at[s, q, i - 1], column(i))

    def c_arrival(s, q, i):
        at = gbuf.at[s, Q * above(Z - i) + q]
        return remote(at, at, c_s.at[s, q, i - 1], c_r.at[s, q, i - 1], column(i))

    def gather(s, q):
        @pl.when(p < 3)
        def _():
            for src in range(2):
                b_arrival(s, q, src).wait_recv()

            def block(j):
                at = lanes(j)
                total = pbuf[s, q, 0, :, at].astype(F32) + pbuf[s, q, 1, :, at].astype(F32)
                gbuf[s, Q * z + q, :, at] = total.astype(BF16)

            loop(W // 128, block)
            for i in (2, 1, 3):
                c_copy(s, q, i).start()

    def gx_copy(s, i):
        to = lax.rem(d + i, DP)
        return remote(
            gbuf.at[s, pl.ds(Q * to, Q)], gcols.at[d, s], gx_s.at[s, i - 1], gx_r.at[s, i - 1], replica(i)
        )

    def gx_arrival(s, i):
        src = lax.rem(d + DP - i, DP)
        return remote(
            gbuf.at[s, pl.ds(0, Q)], gcols.at[src, s], gx_s.at[s, i - 1], gx_r.at[s, i - 1], replica(i)
        )

    def grad_mix(s):
        @pl.when(first)
        def _():
            for i in range(1, T):
                cot_arrival(s, i).wait_recv()

            def block(k):
                rows = crecv[s, :, :, lanes(k, W)].astype(F32)
                gbuf[s, k] = rows.reshape(L, W).astype(BF16)

            loop(B, block)

        for q in range(Q):

            @pl.when(p < 3)
            def _():
                for i in range(1, Z):
                    c_arrival(s, q, i).wait_recv()

            part = None
            for i in range(Z):
                k = Q * above(Z - i) + q
                term = dot(gbuf[s, k], wout[:, lanes(k, W)], NT)
                part = term if part is None else part + term
            if q == 0:
                dyacc[...] = part
            elif q < Q - 1:
                dyacc[...] += part
            else:
                dybf[s] = (dyacc[...] + part).astype(BF16)
        for i in range(1, DP):
            gx_copy(s, i).start()
        gcols[d, s] = gbuf[s, pl.ds(Q * d, Q)]

    def o_copy(s):
        return remote(orow.at[s], gi_v.at[s], o_s.at[s], o_r.at[s], (p + 1, t, d))

    def share(s):
        @pl.when(p < 3)
        def _():
            for k in range(B):
                rows = gbuf[s, k].astype(F32).reshape(T, R, W)
                mine = jnp.where(t == 0, rows[0], 0.0)
                for i in range(1, T):
                    mine = jnp.where(t == i, rows[i], mine)
                orow[s, :, k * W : (k + 1) * W] = mine.astype(BF16)
            o_copy(s).start()

    def pull(s):
        dcb[...] = jnp.zeros_like(dcb)

        def pair(j):
            at = lanes(j)
            dy2 = dybf[s, :, at]
            dm = dot(xst[s, j], dy2, NT)
            dcb[...] += dm[:L] * est[s, j, 0:L, :].astype(F32) + dm[L:] * est[s, j, L : 2 * L, :].astype(F32)
            dx = dot(mt[s, j], dy2, NN)
            dx = jnp.where(iota((L, 128), 1) < 64, dx[:L], dx[L:])
            dx0[s, :, at] = dx
            dcpad[s, 0:L, at] = (dx + skl[:, at] * dy2.astype(F32)) * sp[s, :, at]

        loop(PAIRS, pair)
        low = dcb[...].astype(BF16)
        dcpad[s, 0:L, X : X + N] = dot(low, abf[s, :, X + N : X + 2 * N], NN) * sp[s, :, X : X + N]
        dcpad[s, 0:L, X + N : X + 2 * N] = (
            dot(low, abf[s, :, X : X + N], TN) * sp[s, :, X + N : X + 2 * N]
        )

        def conv(j):
            at = lanes(j)
            du = cw_ref[3:4, at] * dcpad[s, 0:L, at]
            for k in range(3):
                du = du + cw_ref[k : k + 1, at] * dcpad[s, 3 - k : 3 - k + L, at]
            u_ref[0, :, at] = du.astype(BF16)

        loop(C // 128, conv)

    def a_copy(s, q, i):
        return remote(sbuf.at[q, i - 1], rbuf.at[s, q, i - 1], a_s.at[s, q, i - 1], a_r.at[s, q, i - 1], column(i))

    def scatter(s):
        for q in range(Q):
            for i in (2, 1, 3, 0):
                part = dot(u_ref[0], win[lanes(Q * above(i) + q, W), :], NT)
                if i:
                    sbuf[q, i - 1] = part.astype(BF16)
                    a_copy(s, q, i).start()
                else:
                    own[q] = part

    def sent(s):
        for q in range(Q):
            for i in range(1, Z):
                a_copy(s, q, i).wait_send()

    def f_copy(s, i):
        return remote(obuf.at[s, lax.rem(t + i, T)], crecv.at[s, t, :, pl.ds(0, Q * W)], f_s.at[s, i - 1], f_r.at[s, i - 1], peer(i))

    def f_arrival(s, i):
        at = crecv.at[s, lax.rem(t + T - i, T), :, pl.ds(0, Q * W)]
        return remote(obuf.at[s, t], at, f_s.at[s, i - 1], f_r.at[s, i - 1], peer(i))

    def combine(s, q):
        for i in range(1, Z):
            a_copy(s, q, i).wait_recv()

        for j in range(W // 128):
            at = slice(j * 128, (j + 1) * 128)
            mine = side == q // (Q // 2)
            total = own[q, :, at] + jnp.where(mine, gbuf[s, Q * z + q, :, at].astype(F32), 0.0)
            for i in range(Z - 1):
                total = total + rbuf[s, q, i, :, at].astype(F32)
            psum[s, q, :, at] = total.astype(BF16)

            @pl.when(last)
            def _():
                obuf[s, :, :, q * W + j * 128 : q * W + (j + 1) * 128] = total.reshape(T, R, 128).astype(BF16)

        @pl.when(p > 0)
        def _():
            b_copy(s, q, other).start()
            b_copy(s, q, side).start()


    def rows_out(s):
        for i in range(1, T):
            f_copy(s, i).start()
        crecv[s, t, :, 0 : Q * W] = obuf[s, t]

    def parameters(s):
        def two(value):
            high = value.astype(BF16)
            rest = (value - high.astype(F32)).astype(BF16)
            return jnp.concatenate([high, rest], axis=1)

        def pair(j, carry):
            d_s, d_t, d_k = carry
            at = lanes(j)
            dy2 = dybf[s, :, at].astype(F32)
            x2 = abf[s, :, at].astype(F32)
            inner = x2 * dx0[s, :, at]
            outer = dy2 * y0[s, :, at] - inner
            lane = iota((2 * 128, HEADS), 0)
            lane = jnp.where(lane >= 128, lane - 128, lane)
            head = 2 * j + jnp.where(lane >= 64, 1, 0)
            pick = (head == iota((2 * 128, HEADS), 1)).astype(BF16)
            skip = jnp.broadcast_to(jnp.sum(dy2 * x2, axis=0, keepdims=True), (8, 128))
            return (
                d_s + dot(two(outer), pick, NN),
                d_t + dot(two(inner), pick, NN),
                d_k + dot(two(skip), pick, NN),
            )

        zero = jnp.zeros((L, HEADS), F32)
        d_s, d_t, d_k = lax.fori_loop(0, PAIRS, pair, (zero, zero, jnp.zeros((8, HEADS), F32)))
        later = dot((iota((L, L), 0) <= iota((L, L), 1)).astype(F32), d_s, NN, HIGH)
        dt = dtc[s]
        g_al = jnp.sum(later * dt, axis=0, keepdims=True) * rate
        g_db = jnp.sum((d_t / dt + later * rate) * sgc[s], axis=0, keepdims=True)
        small = (g_al, g_db, d_k[0:1])

        def conv(j):
            at = lanes(j)
            dc = dcpad[s, 0:L, at]
            rows = []
            for k in range(4):
                rows.append(jnp.sum(dc * upad[s, TOP - 3 + k : TOP - 3 + k + L, at], axis=0, keepdims=True))
            rows.append(jnp.sum(dc, axis=0, keepdims=True))
            rows.append(jnp.zeros((3, 128), F32))
            value = jnp.concatenate(rows, axis=0)
            pg[:, at] = value if s == 0 else pg[:, at] + value

        loop(C // 128, conv)
        for i in range(3):
            if s == 0:
                pg[5 + i : 6 + i, 0:HEADS] = small[i]
            else:
                pg[5 + i : 6 + i, 0:HEADS] += small[i]

    def pg_copy(i):
        return remote(pg, pgr.at[d], pg_s.at[i - 1], pg_r.at[i - 1], replica(i))

    def pg_arrival(i):
        src = lax.rem(d + DP - i, DP)
        return remote(pg, pgr.at[src], pg_s.at[i - 1], pg_r.at[i - 1], replica(i))

    def projection():
        for s in range(S):
            for i in range(1, DP):
                yb_arrival(s, i).wait_recv()
                gx_arrival(s, i).wait_recv()

        for k in range(2):

            def block(j):
                rows = yb[:, :, :, lanes(j, 256)].reshape(DP * S * L, 256)
                cols = jnp.concatenate(
                    [gcols[:, :, 2 * k + e].reshape(DP * S * L, W) for e in range(2)], axis=1
                )
                win[lanes(j, 256), 2 * k * W : 2 * (k + 1) * W] = dot(rows, cols, TN).astype(BF16)

            loop(X // 256, block)
        local(win.at[pl.ds(0, X), pl.ds(0, X)], gow_out, 3).start()

    dcpad[:, L : L + TOP, :] = jnp.zeros((S, TOP, C), F32)
    for q in range(Q):
        gather(0, q)
    grad_mix(0)
    pull(0)
    local(win_hbm, win, 2).wait()
    scatter(0)
    for q in range(Q):
        gather(1, q)
    for q in range(Q):
        combine(0, q)

    @pl.when(last)
    def _():
        rows_out(0)


    @pl.when(p < 3)
    def _():
        share(0)
        parameters(0)

    grad_mix(1)
    pull(1)
    sent(0)
    scatter(1)

    @pl.when(first)
    def _():
        parameters(0)

    def sum_parameters():
        share(1)
        parameters(1)
        pgr[d] = pg[...]
        for i in range(1, DP):
            pg_copy(i).start()

    @pl.when(last)
    def _():
        sum_parameters()

    for q in range(Q):
        combine(1, q)

    @pl.when(last)
    def _():
        rows_out(1)

    @pl.when(p > 0)
    def _():
        sum_parameters()

    projection()

    for i in range(1, DP):
        pg_arrival(i).wait_recv()
    total = pgr[0]
    for i in range(1, DP):
        total = total + pgr[i]
    pgsum[...] = total
    local(pgsum, pg_out, 4).start()

    @pl.when(last)
    def _():
        for s in range(S):
            for i in range(1, T):
                f_arrival(s, i).wait_recv()
            for k in range(Z):
                a, b = crecv[s, 2 * k, :, 0 : Q * W], crecv[s, 2 * k + 1, :, 0 : Q * W]
                gi_v[s, :, k * Q * W : (k + 1) * Q * W] = (a.astype(F32) + b.astype(F32)).astype(BF16)

    @pl.when(p > 0)
    def _():
        for s in range(S):
            remote(orow.at[s], gi_v.at[s], o_s.at[s], o_r.at[s], (p - 1, t, d)).wait_recv()

    local(gi_v, gi_out, 5).start()

    @pl.when(first)
    def _():
        for s in range(S):
            for i in range(1, T):
                cot_copy(s, i).wait_send()

    @pl.when(p < 3)
    def _():
        for s in range(S):
            o_copy(s).wait_send()
            for q in range(Q):
                for i in range(1, Z):
                    c_copy(s, q, i).wait_send()

    @pl.when(p > 0)
    def _():
        for s in range(S):
            for q in range(Q):
                for to in range(2):
                    b_copy(s, q, to).wait_send()

    @pl.when(last)
    def _():
        for s in range(S):
            for i in range(1, T):
                f_copy(s, i).wait_send()

    for s in range(S):
        for i in range(1, DP):
            yb_copy(s, i).wait_send()
            gx_copy(s, i).wait_send()
    sent(1)
    for i in range(1, DP):
        pg_copy(i).wait_send()
    local(win.at[pl.ds(0, X), pl.ds(0, X)], gow_out, 3).wait()
    local(pgsum, pg_out, 4).wait()
    local(gi_v, gi_out, 5).wait()


def finish(gi_ref, gow_ref, pg_ref, gi, gow, cw, cb, al, db, sk, pg, sems):
    copies = [
        pltpu.make_async_copy(src, dst, sems.at[i])
        for i, (src, dst) in enumerate(((gow_ref, gow), (gi_ref, gi), (pg_ref, pg)))
    ]
    for copy in copies:
        copy.start()
    copies[2].wait()
    cw[...] = pg[0:4, :]
    cb[...] = pg[4:5, :]
    al[...] = pg[5:6, 0:HEADS]
    db[...] = pg[6:7, 0:HEADS]
    sk[...] = pg[7:8, 0:HEADS]
    copies[1].wait()
    copies[0].wait()


def shards(cot, saved_u, dt_raw, in_weight, out_weight, conv_weight, conv_bias, a_log, dt_bias, d_skip):
    any_spec = pl.BlockSpec(memory_space=pl.ANY)
    vmem_spec = pl.BlockSpec(memory_space=pltpu.VMEM)
    sem = pltpu.SemaphoreType.DMA
    scratch = [
        pltpu.VMEM((D, C), BF16),
        pltpu.VMEM((X, D), BF16),
        pltpu.VMEM((S, L, C), BF16),
        pltpu.VMEM((S, L + 2 * TOP, C), F32),
        pltpu.VMEM((S, L, C), F32),
        pltpu.VMEM((S, L, C), BF16),
        pltpu.VMEM((S, PAIRS, 2 * L, 128), BF16),
        pltpu.VMEM((S, PAIRS, 2 * L, L), BF16),
        pltpu.VMEM((S, PAIRS, 2 * L, L), BF16),
        pltpu.VMEM((S, L, X), F32),
        pltpu.VMEM((DP, S, L, X), BF16),
        pltpu.VMEM((HEADS, L), F32),
        pltpu.VMEM((L, HEADS), F32),
        pltpu.VMEM((S, L, HEADS), F32),
        pltpu.VMEM((S, L, HEADS), F32),
        pltpu.VMEM((1, X), F32),
        pltpu.VMEM((S, R, D), BF16),
        pltpu.VMEM((S, T, R, D), BF16),
        pltpu.VMEM((S, B, L, W), BF16),
        pltpu.VMEM((DP, S, Q, L, W), BF16),
        pltpu.VMEM((L, X), F32),
        pltpu.VMEM((S, L, X), BF16),
        pltpu.VMEM((S, L, X), F32),
        pltpu.VMEM((L, L), F32),
        pltpu.VMEM((S, L + TOP, C), F32),
        pltpu.VMEM((Q, L, W), F32),
        pltpu.VMEM((Q, Z - 1, L, W), BF16),
        pltpu.VMEM((S, Q, Z - 1, L, W), BF16),
        pltpu.VMEM((S, Q, L, W), BF16),
        pltpu.VMEM((S, Q, 2, L, W), BF16),
        pltpu.VMEM((S, R, D), BF16),
        pltpu.VMEM((S, T, R, Q * W), BF16),
        pltpu.VMEM((S, R, D), BF16),
        pltpu.VMEM((8, C), F32),
        pltpu.VMEM((DP, 8, C), F32),
        pltpu.VMEM((8, C), F32),
        sem((7,)),
        sem((S, T - 1)), sem((S, T - 1)),
        sem((S, Q, Z - 1)), sem((S, Q, Z - 1)),
        sem((S, Q, 2)), sem((S, Q, 2)),
        sem((S, Q, Z - 1)), sem((S, Q, Z - 1)),
        sem((S, T - 1)), sem((S, T - 1)),
        sem((S,)), sem((S,)),
        sem((S, DP - 1)), sem((S, DP - 1)),
        sem((S, DP - 1)), sem((S, DP - 1)),
        sem((DP - 1,)), sem((DP - 1,)),
    ]
    gi, gow, pg = pl.pallas_call(
        kernel,
        out_shape=(
            jax.ShapeDtypeStruct((S, R, D), BF16),
            jax.ShapeDtypeStruct((X, X), BF16),
            jax.ShapeDtypeStruct((8, C), F32),
        ),
        in_specs=[any_spec, any_spec, any_spec, any_spec] + [vmem_spec] * 6,
        out_specs=(any_spec, any_spec, any_spec),
        scratch_shapes=scratch,
        compiler_params=pltpu.CompilerParams(
            collective_id=0, has_side_effects=True, vmem_limit_bytes=64 * 2**20 - 2**16
        ),
        name="mixer_backward",
    )(cot, saved_u[0], in_weight[0], out_weight[0], jnp.swapaxes(dt_raw[0], 1, 2), conv_weight[0], conv_bias, a_log, dt_bias, d_skip)
    outs = pl.pallas_call(
        finish,
        out_shape=(
            jax.ShapeDtypeStruct((S, R, D), BF16),
            jax.ShapeDtypeStruct((X, X), BF16),
            jax.ShapeDtypeStruct((4, C), F32),
            jax.ShapeDtypeStruct((1, C), F32),
            jax.ShapeDtypeStruct((1, HEADS), F32),
            jax.ShapeDtypeStruct((1, HEADS), F32),
            jax.ShapeDtypeStruct((1, HEADS), F32),
        ),
        in_specs=[any_spec] * 3,
        out_specs=(vmem_spec,) * 7,
        scratch_shapes=[pltpu.VMEM((8, C), F32), sem((3,))],
        compiler_params=pltpu.CompilerParams(vmem_limit_bytes=64 * 2**20 - 2**16),
        name="finish",
    )(gi, gow, pg)
    gi, gow, cw, cb, al, db, sk = outs
    return gi[None], gow[None], cw[None], cb, al, db, sk


def solution(mesh):
    return jax.shard_map(
        shards,
        mesh=mesh,
        in_specs=(
            P("dp", "tensor", None),
            P("pipe", "dp", None, "tensor"),
            P("pipe", "dp", None, "tensor"),
            P("pipe", None, "tensor"),
            P("pipe", "tensor", None),
            P("pipe", None, "tensor"),
            P("pipe", "tensor"),
            P("pipe", "tensor"),
            P("pipe", "tensor"),
            P("pipe", "tensor"),
        ),
        out_specs=(
            P("pipe", "dp", "tensor", None),
            P("pipe", "tensor", "dp"),
            P("pipe", None, "tensor"),
            P("pipe", "tensor"),
            P("pipe", "tensor"),
            P("pipe", "tensor"),
            P("pipe", "tensor"),
        ),
        check_vma=False,
    )
```
